512 devices in a mesh: ctx: 64 (over y_hi, z, core), exp: 8 (over x, y_lo).
Axes of the slice: x: 4, y: 4 (y_hi: 2, y_lo: 2; y = y_hi * 2 + y_lo), z: 16, core: 2. Of those that a mesh axis runs over, the one named last changes fastest.
Arguments:
- normed: bfloat16 [8192, 8192], P('ctx', 'exp'), may hold values from -6 to 6
- frozen_query: bfloat16 [8192, 4096], P('ctx', 'exp'), may hold values from -5 to 5
- input_keys: bfloat16 [8192, 1024], P('ctx', 'exp'), may hold values from -5 to 5
- input_values: bfloat16 [8192, 1024], P('ctx', 'exp'), may hold values from -6 to 6
- document_index: int32 [8192], P('ctx'), may hold values from 0 to 31, never falling along the last dimension, each value on 1 to 5120 neighbouring positions
- routes: int32 [64, 2], P('ctx'), may hold values from 0 to 15, all different within a row
- adapter_down_weight: bfloat16 [16, 8192, 64], P(None, 'exp'), may hold values from -0.0625 to 0.0625
- adapter_up_weight: bfloat16 [1024, 4096], P('ctx', 'exp'), may hold values from -0.75 to 0.75
- output_gradient: bfloat16 [8192, 4096], P('ctx', 'exp'), may hold values from -6 to 6
Outputs:
- attended: float32 [8192, 4096], P('ctx', 'exp')
- query_gradient: float32 [8192, 4096], P('ctx', 'exp')
- key_gradient: float32 [8192, 1024], P('ctx', 'exp')
- value_gradient: float32 [8192, 1024], P('ctx', 'exp')
- up_gradient: float32 [1024, 4096], P('ctx', 'exp')
The draws below stay inside these ranges and needn't reach their ends.
Inputs may be any that keep to these rules, and one draw needn't show every extreme that they name: `document_index`: document ids never fall along the sequence; each document holds 1 to 5120 tokens, and one holds exactly 5120. `routes`: each row names 2 different experts; every expert is named by some row.
All inputs are finite; a program needn't handle non-finite values.
Results may differ from the reference program's by a relative error of at most 0.04.
Values may be sent and summed in bfloat16 or wider, within the bound.
No kernel may reach another device: no remote copies, remote signals or barrier semaphores. Data moves between devices by JAX's collectives and lax.ppermute only.
A program may use at most 64 MiB of HBM per device.

```python
import math
import jax
import jax.numpy as jnp
import numpy as np
from jax import lax

MODEL_WIDTH = 8192
QUERY_HEADS = 32
KEY_VALUE_HEADS = 8
HEAD_SIZE = 128
EXPERT_RANK = 64
EXPERT_COUNT = 16
TOP = 2
BLOCK = 128
TOKEN_COUNT = 8192
MOST = 5120
DOCS = 32


def draw_frozen_query(key, part):
    key = jax.random.fold_in(key, 11)
    base_query = jnp.clip(jax.random.normal(key, (TOKEN_COUNT, KEY_VALUE_HEADS, QUERY_HEADS // KEY_VALUE_HEADS, HEAD_SIZE), jnp.float32), -5.0, 5.0)
    return base_query.reshape(TOKEN_COUNT, QUERY_HEADS * HEAD_SIZE).astype(jnp.bfloat16)


def draw_input_keys(key, part):
    key = jax.random.fold_in(key, 12)
    base_query = jnp.clip(jax.random.normal(key, (TOKEN_COUNT, KEY_VALUE_HEADS, HEAD_SIZE), jnp.float32), -5.0, 5.0)
    return base_query.reshape(TOKEN_COUNT, KEY_VALUE_HEADS * HEAD_SIZE).astype(jnp.bfloat16)


def block_scale(stream_key, shape, split, low, top_value):
    def one(axis_at, parts):
        draws = jax.random.uniform(jax.random.fold_in(jax.random.fold_in(stream_key, 6), axis_at), (parts,), jnp.float32, low / len(split), top_value / len(split))
        return jnp.repeat(jnp.exp(draws), shape[axis_at] // parts).reshape((-1,) + (1,) * (len(shape) - axis_at - 1))

    level = one(*split[0])
    for cut in split[1:]:
        level = level * one(*cut)
    return level


def different_ones(key, rows, number_of, top, lift):
    ranking = jax.random.permutation(jax.random.fold_in(key, 1), number_of)
    boost = ranking
    for power in range(3):
        boost = boost * boost // number_of
    boost = boost * lift // number_of
    chance = jax.random.randint(jax.random.fold_in(key, 2), (rows, number_of), 0, 4096) + boost
    fixed_rows = jax.random.permutation(jax.random.fold_in(key, 3), rows)[jnp.arange(number_of) % rows]
    chance = jnp.where(jnp.arange(rows)[:, None] == fixed_rows[None, :], 1 << 14, chance)
    score = chance * number_of + jnp.arange(number_of)
    return lax.top_k(score.astype(jnp.int32), top)[1].astype(jnp.int32)


def split_up(count, total, limit, skew):
    portions = [(1 << 20) // math.isqrt(rank ** skew) + 1 for rank in range(2, count + 1)]
    spare, counts = total - limit - (count - 1), [1] * (count - 1)
    while spare > 0:
        movable = [i for i in range(count - 1) if counts[i] < limit]
        whole, budget = sum([portions[i] for i in movable]), spare
        for i in movable:
            addition = min(limit - counts[i], max(1, budget * portions[i] // whole), spare)
            counts[i] = counts[i] + addition
            spare = spare - addition
    return np.array([limit] + counts)


def uneven_parts(own_key, count, total, bound, lean):
    if count == 2:
        one = jax.random.randint(own_key, (), max(1, total - bound), min(bound, total - 1) + 1)
        return jnp.stack([one, total - one])
    lengths = jnp.asarray(split_up(count, total, bound, lean), jnp.int32)
    twos = (count - 1) // 2
    giver, sink = lengths[1:1 + 2 * twos:2], lengths[2:2 + 2 * twos:2]
    slack = jnp.minimum(giver - 1, bound - sink)
    moved = jax.random.randint(jax.random.fold_in(own_key, 1), (twos,), 0, 1 << 20) % (slack + 1)
    lengths = lengths.at[1:1 + 2 * twos:2].set(giver - moved).at[2:2 + 2 * twos:2].set(sink + moved)
    return lengths[jax.random.permutation(jax.random.fold_in(own_key, 2), count)]


def centred(rng, shape, scale, bound, split=(), kind=jnp.bfloat16):
    values = jax.random.normal(rng, shape, jnp.float32) * scale
    if len(split) > 0:
        values = block_scale(rng, shape, split, -0.22, 0.18) * values
    return jnp.clip(values, min=-bound, max=bound).astype(kind)


def setup_inputs(seed: int = 0) -> dict:
    streams_of = jax.random.split(jax.random.key(seed), 10)
    return {
        "normed": centred(streams_of[0], (TOKEN_COUNT, MODEL_WIDTH), 1.0, 6.0, ((0, 64), (1, 8))),
        "frozen_query": draw_frozen_query(jax.random.fold_in(streams_of[9], 71), 0),
        "input_keys": draw_input_keys(jax.random.fold_in(streams_of[9], 71), 0),
        "input_values": centred(streams_of[3], (TOKEN_COUNT, KEY_VALUE_HEADS * HEAD_SIZE), 1.0, 6.0, ((0, 64), (1, 8))),
        "document_index": jnp.searchsorted(jnp.cumsum(uneven_parts(streams_of[4], DOCS, TOKEN_COUNT, MOST, 2)), jnp.arange(TOKEN_COUNT), side="right").astype(jnp.int32),
        "routes": different_ones(streams_of[5], (TOKEN_COUNT // BLOCK), EXPERT_COUNT, TOP, 2048),
        "adapter_down_weight": centred(streams_of[6], (EXPERT_COUNT, MODEL_WIDTH, EXPERT_RANK), MODEL_WIDTH ** -0.5, 0.0625, ((1, 8),)),
        "adapter_up_weight": centred(streams_of[7], (EXPERT_COUNT * EXPERT_RANK, QUERY_HEADS * HEAD_SIZE), EXPERT_RANK ** -0.5, 0.75, ((0, 64), (1, 8))),
        "output_gradient": centred(streams_of[8], (TOKEN_COUNT, QUERY_HEADS * HEAD_SIZE), 1.0, 6.0, ((0, 64), (1, 8))),
    }


adapter_scale = 0.5
far_below = -1e+30

def reference(normed, frozen_query, input_keys, input_values, document_index, routes, adapter_down_weight, adapter_up_weight, output_gradient):
    inverse = 1.0 / math.sqrt(HEAD_SIZE)
    block_total = TOKEN_COUNT // BLOCK
    row_blocks = normed.reshape(block_total, BLOCK, MODEL_WIDTH)

    def down_block(pair):
        block_rows, chosen_experts = pair
        expert_factors = adapter_down_weight[chosen_experts].astype(jnp.float32)
        return jnp.einsum('nd,jdr->njr', block_rows.astype(jnp.float32), expert_factors)
    low_rank = lax.map(down_block, (row_blocks, routes)).astype(jnp.bfloat16)
    selector = (routes[:, :, None] == jnp.arange(EXPERT_COUNT, dtype=jnp.int32)[None, None, :]).astype(jnp.float32)
    reduced_full = jnp.einsum('bnjr,bje->bner', low_rank.astype(jnp.float32), selector)
    reduced_full = reduced_full.reshape(TOKEN_COUNT, EXPERT_COUNT * EXPERT_RANK).astype(jnp.bfloat16)
    query_rows = (frozen_query.astype(jnp.float32) + adapter_scale * jnp.dot(reduced_full, adapter_up_weight, preferred_element_type=jnp.float32)).astype(jnp.bfloat16)
    heads_per_group = QUERY_HEADS // KEY_VALUE_HEADS
    positions = jnp.arange(TOKEN_COUNT, dtype=jnp.int32)
    allowed = (document_index[:, None] == document_index[None, :]) & (positions[None, :] <= positions[:, None])
    query_heads = query_rows.reshape(TOKEN_COUNT, QUERY_HEADS, HEAD_SIZE).transpose(1, 0, 2)
    out_heads = output_gradient.reshape(TOKEN_COUNT, QUERY_HEADS, HEAD_SIZE).transpose(1, 0, 2)
    key_head_rows = input_keys.reshape(TOKEN_COUNT, KEY_VALUE_HEADS, HEAD_SIZE).transpose(1, 0, 2)
    value_head_rows = input_values.reshape(TOKEN_COUNT, KEY_VALUE_HEADS, HEAD_SIZE).transpose(1, 0, 2)

    def one_head(head):
        query_h = query_heads[head]
        key_g = key_head_rows[head // heads_per_group]
        value_g = value_head_rows[head // heads_per_group]
        dout = out_heads[head]
        score = jnp.dot(query_h, key_g.T, preferred_element_type=jnp.float32) * inverse
        top = lax.optimization_barrier(jnp.max(jnp.where(allowed, score, far_below), axis=1, keepdims=True))
        expo = jnp.where(allowed, jnp.exp(score - top), 0.0)
        prob = expo / lax.optimization_barrier(jnp.sum(expo, axis=1, keepdims=True))
        prob_low = prob.astype(jnp.bfloat16)
        attended_full = jnp.dot(prob_low, value_g, preferred_element_type=jnp.float32)
        attended_low = attended_full.astype(jnp.bfloat16)
        row_delta = lax.optimization_barrier(jnp.sum(dout.astype(jnp.float32) * attended_low.astype(jnp.float32), axis=1, keepdims=True))
        dprob = jnp.dot(dout, value_g.T, preferred_element_type=jnp.float32)
        dscore = (prob * (dprob - row_delta)).astype(jnp.bfloat16)
        dquery = jnp.dot(dscore, key_g, preferred_element_type=jnp.float32) * inverse
        dkey = jnp.dot(dscore.T, query_h, preferred_element_type=jnp.float32) * inverse
        dvalue = jnp.dot(prob_low.T, dout, preferred_element_type=jnp.float32)
        return (attended_full, dquery, dkey, dvalue)
    attended_all, dquery_all, key_gradient_total, value_gradient_total = lax.map(one_head, jnp.arange(QUERY_HEADS, dtype=jnp.int32))
    attended = attended_all.transpose(1, 0, 2).reshape(TOKEN_COUNT, QUERY_HEADS * HEAD_SIZE)
    query_gradient = dquery_all.transpose(1, 0, 2).reshape(TOKEN_COUNT, QUERY_HEADS * HEAD_SIZE)
    query_low = query_gradient.astype(jnp.bfloat16)
    key_gradient = key_gradient_total.reshape(KEY_VALUE_HEADS, heads_per_group, TOKEN_COUNT, HEAD_SIZE).sum(axis=1)
    key_gradient = key_gradient.transpose(1, 0, 2).reshape(TOKEN_COUNT, KEY_VALUE_HEADS * HEAD_SIZE)
    value_gradient = value_gradient_total.reshape(KEY_VALUE_HEADS, heads_per_group, TOKEN_COUNT, HEAD_SIZE).sum(axis=1)
    value_gradient = value_gradient.transpose(1, 0, 2).reshape(TOKEN_COUNT, KEY_VALUE_HEADS * HEAD_SIZE)
    up_gradient = adapter_scale * jnp.dot(reduced_full.T, query_low, preferred_element_type=jnp.float32)
    return (attended, query_gradient, key_gradient, value_gradient, up_gradient)
```

```python
import functools
import math

import jax
import jax.numpy as jnp
from jax import lax
from jax.experimental import pallas as pl
from jax.experimental.pallas import tpu as pltpu
from jax.sharding import PartitionSpec as P

HEAD = 128
RANK = 64
BLOCK = 128
QUAD = 4 * BLOCK

adapter_scale = 0.5
far_below = -1e30
to_two = math.log2(math.e) / math.sqrt(HEAD)
inverse = 1.0 / math.sqrt(HEAD)
f32 = jnp.float32
bf16 = jnp.bfloat16

KV = 2 * BLOCK
UPS = 64
GRAD = KV + 2 * UPS
PACK = GRAD + 16
KEYS, VALUES = slice(0, BLOCK), slice(BLOCK, KV)


def last_last(a, b):
    return lax.dot_general(a, b, (((1,), (1,)), ((), ())), preferred_element_type=f32)


def first_first(a, b):
    return lax.dot_general(a, b, (((0,), (0,)), ((), ())), preferred_element_type=f32)


def plain(a, b):
    return lax.dot_general(a, b, (((1,), (0,)), ((), ())), preferred_element_type=f32)


def sum_low(lows, low_out):
    low = lows[0]
    for i in range(1, lows.shape[0]):
        low = low + lows[i]
    low_out[...] = low.astype(bf16)


def prepare(heads, pair, docs, frozen_out, gout_t, pick):
    lane = lax.broadcasted_iota(jnp.int32, (128, BLOCK), 0)
    for w in range(2):
        for h in range(heads):
            columns = slice(h * HEAD, (h + 1) * HEAD)
            frozen_out[w, h * BLOCK : (h + 1) * BLOCK, :] = pair[w, 0:BLOCK, columns]
            gout_t[w, :, columns] = pair[w, BLOCK : 2 * BLOCK, columns].astype(f32).T
        pick[w] = jnp.where(lane == docs[w, 0:1, :], 1.0, 0.0).astype(bf16)


def expert_at(meta, z_count, w, j):
    first = meta[3 + 2 * w + j] * 4
    return lax.rem(first, 2 * z_count) // 2, lax.div(first, 2 * z_count) ^ meta[0]


def query_base(meta, z_count, w):
    yh, z, core = meta[0], meta[1], meta[2]
    across = (1 - 2 * yh) * 2 * z_count * BLOCK
    return (2 * z + core) * BLOCK + w * across


def quad_range(meta, z_count, w, start):
    base = query_base(meta, z_count, w)
    first_key = jnp.min(start.astype(f32)).astype(jnp.int32)
    first = jnp.clip(first_key, 0, z_count * KV) // QUAD
    last = jnp.clip(base, -QUAD, z_count * KV - 1) // QUAD
    last = jnp.where(base < 0, -1, last)
    return first, last


def chip_pieces(core, own, other, quad):
    z_at = quad * 2
    return [
        (own, z_at, core),
        (other, z_at, 1 - core),
        (own, z_at + 1, 2 + core),
        (other, z_at + 1, 3 - core),
    ]


def rows_of(n):
    return slice(n * BLOCK, (n + 1) * BLOCK)


def forward(
    heads,
    z_count,
    meta,
    own,
    other,
    low_ref,
    frozen,
    pick_ref,
    query,
    start_out,
    prob,
    out_ref,
    stats,
    payload,
    score,
):
    wide = heads * BLOCK
    yh, core = meta[0], meta[2]

    for w in range(2):
        low = low_ref[w]
        for h in range(heads):
            rows = []
            for j in range(2):
                z_at, slot = expert_at(meta, z_count, w, j)
                at = pl.ds(pl.multiple_of(KV + slot * UPS + 16 * h, 16), 16)
                for step in range(2):
                    mine, theirs = own[z_at + step, at, :], other[z_at + step, at, :]
                    rows.append(jnp.where(core == 0, mine, theirs))
                    rows.append(jnp.where(core == 0, theirs, mine))
            delta = plain(low, jnp.concatenate(rows, axis=0))
            block = slice(h * BLOCK, (h + 1) * BLOCK)
            query[w, block, :] = (
                frozen[w, block, :].astype(f32) + adapter_scale * delta
            ).astype(bf16)

    counts = jnp.zeros((16, 128), f32)
    for i in range(z_count):
        counts += own[i, GRAD:PACK, :].astype(f32) + other[i, GRAD:PACK, :].astype(f32)
    high = jnp.floor(counts * (1.0 / 128.0))
    rest = counts - 128.0 * high
    high, rest = high.astype(bf16), rest.astype(bf16)
    ramp = lax.broadcasted_iota(jnp.int32, (BLOCK, wide), 0)

    for w in range(2):
        pick = pick_ref[w]
        start = jnp.sum(128.0 * plain(high, pick) + plain(rest, pick), axis=0, keepdims=True)
        start = start.astype(jnp.int32) - yh * (z_count * KV)
        whole_key = jnp.max(start.astype(f32)).astype(jnp.int32)
        first_quad, last_quad = quad_range(meta, z_count, w, start)
        start = jnp.concatenate([start] * heads, axis=1)
        start_out[w] = jnp.broadcast_to(start, (8, wide))
        place = query_base(meta, z_count, w) + lax.broadcasted_iota(jnp.int32, (1, BLOCK), 1)
        place = jnp.concatenate([place] * heads, axis=1)
        whole_key = jnp.clip(whole_key, 0, z_count * KV)
        whole_quad = jnp.minimum(
            jnp.maximum((whole_key + QUAD - 1) // QUAD, first_quad), last_quad
        )
        queries = query[w]

        def scores(masked, quad, top):
            for n, (src, z_at, at) in enumerate(chip_pieces(core, own, other, quad)):
                s = last_last(src[z_at, KEYS, :], queries)
                if masked:
                    base = quad * QUAD + at * BLOCK
                    s = jnp.where((ramp >= start - base) & (ramp <= place - base), s, far_below)
                score[quad, rows_of(n), :] = s
                top = jnp.maximum(top, jnp.max(s.reshape(BLOCK // 8, 8, wide), axis=0))
            return top

        top = jnp.full((8, wide), far_below, f32)
        top = lax.fori_loop(
            first_quad,
            jnp.where(last_quad >= first_quad, whole_quad + 1, first_quad),
            lambda i, t: scores(True, jnp.where(i == whole_quad, last_quad, i), t),
            top,
        )
        top = lax.fori_loop(
            jnp.maximum(whole_quad, first_quad),
            last_quad,
            functools.partial(scores, False),
            top,
        )
        top = jnp.max(top, axis=0, keepdims=True)
        top = jnp.where(top < 0.5 * far_below, 0.0, top)

        def attend(quad, carry):
            total, out = carry
            values = []
            for n, (src, z_at, _) in enumerate(chip_pieces(core, own, other, quad)):
                p = jnp.exp2((score[quad, rows_of(n), :] - top) * to_two)
                total = total + jnp.sum(p.reshape(BLOCK // 8, 8, wide), axis=0)
                prob[w, quad, rows_of(n), :] = p.astype(bf16)
                values.append(src[z_at, VALUES, :])
            out = out + first_first(jnp.concatenate(values, axis=0), prob[w, quad])
            return total, out

        total, out = lax.fori_loop(
            first_quad,
            last_quad + 1,
            attend,
            (jnp.zeros((8, wide), f32), jnp.zeros((HEAD, wide), f32)),
        )
        total = jnp.sum(total, axis=0, keepdims=True)
        some = total > 0.0
        safe = jnp.where(some, total, 1.0)
        out_ref[w] = out * (1.0 / safe)
        log_top = top * to_two
        log_sum = jnp.where(some, log_top + jnp.log2(safe), far_below)
        filled = jnp.where(some, 1.0, 0.0)
        stats[w] = jnp.concatenate(
            [log_top, log_sum, filled, jnp.zeros((5, wide), f32)], axis=0
        )

    cross = 1 - yh
    payload[0:HEAD, :] = out_ref[cross].astype(bf16)
    log_sum = stats[cross, 1:2, :]
    high = log_sum.astype(bf16)
    rest = log_sum - high.astype(f32)
    mid = rest.astype(bf16)
    low = (rest - mid.astype(f32)).astype(bf16)
    payload[HEAD : HEAD + 16, :] = jnp.concatenate(
        [high, mid, low, jnp.zeros((13, wide), bf16)], axis=0
    )


def backward(
    heads,
    z_count,
    meta,
    own,
    other,
    query,
    start_ref,
    prob,
    out_ref,
    stats,
    come,
    gout_t,
    low_ref,
    attended,
    dquery,
    dquery_across,
    send_own,
    send_other,
    sum_own,
    sum_other,
    gscaled,
):
    wide = heads * BLOCK
    yh, core = meta[0], meta[2]
    sum_own[...] = jnp.zeros(sum_own.shape, f32)
    sum_other[...] = jnp.zeros(sum_other.shape, f32)
    send_own[:, KV:GRAD, :] = jnp.zeros((z_count, 2 * UPS, HEAD), bf16)
    send_other[:, KV:GRAD, :] = jnp.zeros((z_count, 2 * UPS, HEAD), bf16)
    pieces = come[HEAD : HEAD + 16, :].astype(f32)
    come_log = pieces[0:1] + pieces[1:2] + pieces[2:3]

    for w in range(2):
        crossed = (1 - yh) == w
        log_top, log_sum, filled = (stats[w, i : i + 1, :] for i in range(3))
        far_log = jnp.where(crossed, come_log, far_below)
        most = jnp.maximum(log_sum, far_log)
        log_all = most + jnp.log2(jnp.exp2(log_sum - most) + jnp.exp2(far_log - most))
        far_share = jnp.where(crossed, jnp.exp2(far_log - log_all), 0.0)
        out = (
            out_ref[w] * jnp.exp2(log_sum - log_all)
            + come[0:HEAD, :].astype(f32) * far_share
        )
        scale = jnp.where(filled > 0.0, jnp.exp2(log_top - log_all), 0.0)
        gout = gout_t[w]
        delta = jnp.sum(gout * out.astype(bf16).astype(f32), axis=0, keepdims=True) * scale
        gout = gout * scale
        for h in range(heads):
            columns = slice(h * HEAD, (h + 1) * HEAD)
            if w == 0:
                attended[:, columns] = out[:, columns].T
            gscaled[h * BLOCK : (h + 1) * BLOCK, :] = gout[:, columns].T.astype(bf16)
        grads = gscaled[...]
        queries = query[w]
        first_quad, last_quad = quad_range(meta, z_count, w, start_ref[w])

        def step(quad, dq):
            keys, dscores = [], []
            places = chip_pieces(core, (own, sum_own), (other, sum_other), quad)
            for n, ((src, dst), z_at, _) in enumerate(places):
                p = prob[w, quad, rows_of(n), :]
                dp = last_last(src[z_at, VALUES, :], grads)
                ds = (p.astype(f32) * (dp - delta)).astype(bf16)
                dst[z_at, KEYS, :] += plain(ds, queries)
                dst[z_at, VALUES, :] += plain(p, grads)
                keys.append(src[z_at, KEYS, :])
                dscores.append(ds)
            return dq + first_first(
                jnp.concatenate(keys, axis=0), jnp.concatenate(dscores, axis=0)
            )

        dq = lax.fori_loop(first_quad, last_quad + 1, step, jnp.zeros((HEAD, wide), f32))
        dq = dq * inverse
        low = low_ref[w]
        for h in range(heads):
            columns = slice(h * HEAD, (h + 1) * HEAD)
            dq_h = dq[:, columns].T
            dq_low = dq_h.astype(bf16)
            if w == 0:
                dquery[:, columns] = dq_h
            else:
                dquery_across[:, columns] = dq_low
            up = adapter_scale * first_first(low, dq_low)
            for j in range(2):
                z_at, slot = expert_at(meta, z_count, w, j)
                at = pl.ds(pl.multiple_of(KV + slot * UPS + 16 * h, 16), 16)
                for i in range(2):
                    row = j * RANK + 32 * i
                    even, odd = up[row : row + 16, :], up[row + 16 : row + 32, :]
                    for ref, part in (
                        (send_own, jnp.where(core == 0, even, odd)),
                        (send_other, jnp.where(core == 0, odd, even)),
                    ):
                        ref[z_at + i, at, :] = (
                            ref[z_at + i, at, :].astype(f32) + part
                        ).astype(bf16)

    for src, dst in ((sum_own, send_own), (sum_other, send_other)):
        dst[:, KEYS, :] = (src[:, KEYS, :] * inverse).astype(bf16)
        dst[:, VALUES, :] = src[:, VALUES, :].astype(bf16)


def swap(array, distance):
    count = lax.axis_size("ctx")
    return lax.ppermute(array, "ctx", [(i, i ^ distance) for i in range(count)])


def shards(
    normed,
    frozen_query,
    input_keys,
    input_values,
    document_index,
    routes,
    adapter_down_weight,
    adapter_up_weight,
    output_gradient,
):
    z_count = lax.axis_size("ctx") // 4
    across = 2 * z_count
    exp_count = lax.axis_size("exp")
    place = lax.axis_index("ctx")
    runs = [
        [(yh * z_count + z) * 2 + core for z in range(z_count)]
        for yh in range(2)
        for core in range(2)
    ]
    rows = normed.shape[0]
    wide = frozen_query.shape[1]
    heads = wide // HEAD
    stack = heads * rows
    up_rows = adapter_up_weight.shape[0]
    vmem = pl.BlockSpec(memory_space=pltpu.VMEM)
    smem = pl.BlockSpec(memory_space=pltpu.SMEM)

    ups = adapter_up_weight.reshape(up_rows, heads, HEAD).transpose(1, 0, 2)
    ups = ups.reshape(up_rows * heads, HEAD)
    lower = document_index[:, None] < jnp.arange(128, dtype=jnp.int32)[None, :]
    counts = jnp.sum(lower.astype(f32), axis=0, keepdims=True).astype(bf16)
    small = jnp.concatenate([ups, jnp.pad(counts, ((0, 15), (0, 0)))], axis=0)
    small_across = swap(small, across)
    pack = jnp.concatenate(
        [
            input_keys,
            input_values,
            ups,
            small_across[:UPS],
            small[UPS:] + small_across[UPS:],
        ],
        axis=0,
    )
    own = lax.all_gather(pack, "ctx", axis=0, tiled=False, axis_index_groups=runs)

    chosen = [
        lax.dynamic_index_in_dim(adapter_down_weight, routes[0, j], 0, keepdims=False)
        for j in range(2)
    ]
    partial = jnp.dot(normed, jnp.concatenate(chosen, axis=1), preferred_element_type=f32)
    lows = lax.all_to_all(
        jnp.broadcast_to(partial[None], (exp_count,) + partial.shape), "exp", 0, 0
    )
    low = pl.pallas_call(
        sum_low,
        out_shape=jax.ShapeDtypeStruct(partial.shape, bf16),
        in_specs=[vmem],
        out_specs=vmem,
    )(lows)
    low = jnp.stack([low, swap(low, across)])
    local = jnp.concatenate([frozen_query, output_gradient], axis=0)
    local, _ = lax.optimization_barrier((local, pack))
    pair = jnp.stack([local, swap(local, across)])
    ints = jnp.concatenate(
        [document_index.reshape(1, rows), jnp.pad(routes, ((0, 7 - 1), (0, rows - 2)))], axis=0
    )
    ints, _ = lax.optimization_barrier((ints, pack))
    ints = jnp.stack([ints, swap(ints, across)])
    frozen, gout_t, pick = pl.pallas_call(
        functools.partial(prepare, heads),
        out_shape=(
            jax.ShapeDtypeStruct((2, stack, HEAD), bf16),
            jax.ShapeDtypeStruct((2, HEAD, stack), f32),
            jax.ShapeDtypeStruct((2, 128, rows), bf16),
        ),
        in_specs=[vmem] * 2,
        out_specs=(vmem,) * 3,
    )(pair, ints)
    meta = jnp.stack(
        [
            place // across,
            place // 2 % z_count,
            place % 2,
            ints[0, 1, 0],
            ints[0, 1, 1],
            ints[1, 1, 0],
            ints[1, 1, 1],
        ]
    ).astype(jnp.int32)
    own, low, frozen, gout_t, pick, meta = lax.optimization_barrier(
        (own, low, frozen, gout_t, pick, meta)
    )
    other = swap(own, 1)

    quads = z_count // 2
    query, start, prob, out, stats, payload = pl.pallas_call(
        functools.partial(forward, heads, z_count),
        out_shape=(
            jax.ShapeDtypeStruct((2, stack, HEAD), bf16),
            jax.ShapeDtypeStruct((2, 8, stack), jnp.int32),
            jax.ShapeDtypeStruct((2, quads, QUAD, stack), bf16),
            jax.ShapeDtypeStruct((2, HEAD, stack), f32),
            jax.ShapeDtypeStruct((2, 8, stack), f32),
            jax.ShapeDtypeStruct((HEAD + 16, stack), bf16),
        ),
        in_specs=[smem] + [vmem] * 5,
        out_specs=(vmem,) * 6,
        scratch_shapes=[pltpu.VMEM((quads, QUAD, stack), f32)],
        compiler_params=pltpu.CompilerParams(vmem_limit_bytes=30 * 1024 * 1024),
    )(meta, own, other, low, frozen, pick)
    come = swap(payload, across)

    send = jax.ShapeDtypeStruct((z_count, GRAD, HEAD), bf16)
    attended, dquery, dquery_across, send_own, send_other = pl.pallas_call(
        functools.partial(backward, heads, z_count),
        out_shape=(
            jax.ShapeDtypeStruct((rows, wide), f32),
            jax.ShapeDtypeStruct((rows, wide), f32),
            jax.ShapeDtypeStruct((rows, wide), bf16),
            send,
            send,
        ),
        in_specs=[smem] + [vmem] * 10,
        out_specs=(vmem,) * 5,
        scratch_shapes=[
            pltpu.VMEM((z_count, KV, HEAD), f32),
            pltpu.VMEM((z_count, KV, HEAD), f32),
            pltpu.VMEM((stack, HEAD), bf16),
        ],
        compiler_params=pltpu.CompilerParams(vmem_limit_bytes=30 * 1024 * 1024),
    )(meta, own, other, query, start, prob, out, stats, come, gout_t, low)

    chip = send_own + swap(send_other, 1)
    grads = lax.psum_scatter(
        chip, "ctx", scatter_dimension=0, tiled=False, axis_index_groups=runs
    )
    dquery_across, _ = lax.optimization_barrier((dquery_across, chip))
    dquery = dquery + swap(dquery_across, across).astype(f32)
    up_grad = grads[KV : KV + UPS].astype(f32) + swap(grads[KV + UPS :], across).astype(f32)
    up_grad = up_grad.reshape(heads, up_rows, HEAD).transpose(1, 0, 2)
    return (
        attended,
        dquery,
        grads[KEYS].astype(f32),
        grads[VALUES].astype(f32),
        up_grad.reshape(up_rows, wide),
    )


def solution(mesh):
    both = P("ctx", "exp")
    return jax.shard_map(
        shards,
        mesh=mesh,
        in_specs=(
            both,
            both,
            both,
            both,
            P("ctx"),
            P("ctx", None),
            P(None, "exp", None),
            both,
            both,
        ),
        out_specs=(both,) * 5,
        check_vma=False,
    )
```

```python
import functools
import math

import jax
import jax.numpy as jnp
from jax import lax
from jax.experimental import pallas as pl
from jax.experimental.pallas import tpu as pltpu
from jax.sharding import PartitionSpec as P

HEAD = 128
RANK = 64
BLOCK = 128
QUAD = 4 * BLOCK

adapter_scale = 0.5
far_below = -1e30
to_two = math.log2(math.e) / math.sqrt(HEAD)
inverse = 1.0 / math.sqrt(HEAD)
f32 = jnp.float32
bf16 = jnp.bfloat16

KV = 2 * BLOCK
UPS = 64
GRAD = KV + 2 * UPS
HALF = GRAD // 2
PACK = GRAD + 16
KEYS, VALUES = slice(0, BLOCK), slice(BLOCK, KV)


def last_last(a, b):
    return lax.dot_general(a, b, (((1,), (1,)), ((), ())), preferred_element_type=f32)


def first_first(a, b):
    return lax.dot_general(a, b, (((0,), (0,)), ((), ())), preferred_element_type=f32)


def plain(a, b):
    return lax.dot_general(a, b, (((1,), (0,)), ((), ())), preferred_element_type=f32)


def sum_low(lows, low_out):
    low = lows[0]
    for i in range(1, lows.shape[0]):
        low = low + lows[i]
    low_out[...] = low.astype(bf16)


def prepare(heads, pair, docs, frozen_out, gout_t, pick):
    lane = lax.broadcasted_iota(jnp.int32, (128, BLOCK), 0)
    for w in range(2):
        for h in range(heads):
            columns = slice(h * HEAD, (h + 1) * HEAD)
            frozen_out[w, h * BLOCK : (h + 1) * BLOCK, :] = pair[w, 0:BLOCK, columns]
            gout_t[w, :, columns] = pair[w, BLOCK : 2 * BLOCK, columns].astype(f32).T
        pick[w] = jnp.where(lane == docs[w, 0:1, :], 1.0, 0.0).astype(bf16)


def expert_at(meta, z_count, w, j):
    first = meta[3 + 2 * w + j] * 4
    return lax.rem(first, 2 * z_count) // 2, lax.div(first, 2 * z_count) ^ meta[0]


def query_base(meta, z_count, w):
    yh, z, core = meta[0], meta[1], meta[2]
    across = (1 - 2 * yh) * 2 * z_count * BLOCK
    return (2 * z + core) * BLOCK + w * across


def quad_range(meta, z_count, w, start):
    base = query_base(meta, z_count, w)
    first_key = jnp.min(start.astype(f32)).astype(jnp.int32)
    first = jnp.clip(first_key, 0, z_count * KV) // QUAD
    last = jnp.clip(base, -QUAD, z_count * KV - 1) // QUAD
    last = jnp.where(base < 0, -1, last)
    return first, last


def chip_pieces(core, own, other, quad):
    z_at = quad * 2
    return [
        (own, z_at, core),
        (other, z_at, 1 - core),
        (own, z_at + 1, 2 + core),
        (other, z_at + 1, 3 - core),
    ]


def rows_of(n):
    return slice(n * BLOCK, (n + 1) * BLOCK)


def forward(
    heads,
    z_count,
    meta,
    own,
    other,
    low_ref,
    frozen,
    pick_ref,
    gout_t,
    query,
    start_out,
    prob,
    out_ref,
    stats,
    score,
):
    wide = heads * BLOCK
    yh, core = meta[0], meta[2]

    for w in range(2):
        low = low_ref[w]
        for h in range(heads):
            rows = []
            for j in range(2):
                z_at, slot = expert_at(meta, z_count, w, j)
                at = pl.ds(pl.multiple_of(KV + slot * UPS + 16 * h, 16), 16)
                for step in range(2):
                    mine, theirs = own[z_at + step, at, :], other[z_at + step, at, :]
                    rows.append(jnp.where(core == 0, mine, theirs))
                    rows.append(jnp.where(core == 0, theirs, mine))
            delta = plain(low, jnp.concatenate(rows, axis=0))
            block = slice(h * BLOCK, (h + 1) * BLOCK)
            query[w, block, :] = (
                frozen[w, block, :].astype(f32) + adapter_scale * delta
            ).astype(bf16)

    counts = jnp.zeros((16, 128), f32)
    for i in range(z_count):
        counts += own[i, GRAD:PACK, :].astype(f32) + other[i, GRAD:PACK, :].astype(f32)
    high = jnp.floor(counts * (1.0 / 128.0))
    rest = counts - 128.0 * high
    high, rest = high.astype(bf16), rest.astype(bf16)
    ramp = lax.broadcasted_iota(jnp.int32, (BLOCK, wide), 0)

    for w in range(2):
        pick = pick_ref[w]
        start = jnp.sum(128.0 * plain(high, pick) + plain(rest, pick), axis=0, keepdims=True)
        start = start.astype(jnp.int32) - yh * (z_count * KV)
        whole_key = jnp.max(start.astype(f32)).astype(jnp.int32)
        first_quad, last_quad = quad_range(meta, z_count, w, start)
        start = jnp.concatenate([start] * heads, axis=1)
        start_out[w] = jnp.broadcast_to(start, (8, wide))
        place = query_base(meta, z_count, w) + lax.broadcasted_iota(jnp.int32, (1, BLOCK), 1)
        place = jnp.concatenate([place] * heads, axis=1)
        whole_key = jnp.clip(whole_key, 0, z_count * KV)
        whole_quad = jnp.minimum(
            jnp.maximum((whole_key + QUAD - 1) // QUAD, first_quad), last_quad
        )
        queries = query[w]

        def scores(masked, quad, top):
            for n, (src, z_at, at) in enumerate(chip_pieces(core, own, other, quad)):
                s = last_last(src[z_at, KEYS, :], queries)
                if masked:
                    base = quad * QUAD + at * BLOCK
                    s = jnp.where((ramp >= start - base) & (ramp <= place - base), s, far_below)
                score[quad, rows_of(n), :] = s
                top = jnp.maximum(top, jnp.max(s.reshape(BLOCK // 8, 8, wide), axis=0))
            return top

        top = jnp.full((8, wide), far_below, f32)
        top = lax.fori_loop(
            first_quad,
            jnp.where(last_quad >= first_quad, whole_quad + 1, first_quad),
            lambda i, t: scores(True, jnp.where(i == whole_quad, last_quad, i), t),
            top,
        )
        top = lax.fori_loop(
            jnp.maximum(whole_quad, first_quad),
            last_quad,
            functools.partial(scores, False),
            top,
        )
        top = jnp.max(top, axis=0, keepdims=True)
        top = jnp.where(top < 0.5 * far_below, 0.0, top)

        def attend(quad, carry):
            total, out = carry
            values = []
            for n, (src, z_at, _) in enumerate(chip_pieces(core, own, other, quad)):
                p = jnp.exp2((score[quad, rows_of(n), :] - top) * to_two)
                total = total + jnp.sum(p.reshape(BLOCK // 8, 8, wide), axis=0)
                prob[w, quad, rows_of(n), :] = p.astype(bf16)
                values.append(src[z_at, VALUES, :])
            out = out + first_first(jnp.concatenate(values, axis=0), prob[w, quad])
            return total, out

        total, out = lax.fori_loop(
            first_quad,
            last_quad + 1,
            attend,
            (jnp.zeros((8, wide), f32), jnp.zeros((HEAD, wide), f32)),
        )
        total = jnp.sum(total, axis=0, keepdims=True)
        some = total > 0.0
        safe = jnp.where(some, total, 1.0)
        out = out * (1.0 / safe)
        out_ref[w] = out
        row_delta = jnp.sum(gout_t[w] * out, axis=0, keepdims=True)
        log_top = top * to_two
        log_sum = jnp.where(some, log_top + jnp.log2(safe), far_below)
        filled = jnp.where(some, 1.0, 0.0)
        stats[w] = jnp.concatenate(
            [log_sum, row_delta, log_top, filled, jnp.zeros((4, wide), f32)], axis=0
        )


def shares(log_sum, far_log, crossed):
    far_log = jnp.where(crossed, far_log, far_below)
    most = jnp.maximum(log_sum, far_log)
    log_all = most + jnp.log2(jnp.exp2(log_sum - most) + jnp.exp2(far_log - most))
    far = jnp.where(crossed, jnp.exp2(far_log - log_all), 0.0)
    return log_all, jnp.exp2(log_sum - log_all), far


def backward(
    heads,
    z_count,
    meta,
    own,
    other,
    query,
    start_ref,
    prob,
    stats,
    come,
    gout_t,
    low_ref,
    dquery,
    dquery_across,
    to_own_a,
    to_own_b,
    to_mine_a,
    to_mine_b,
    to_theirs_a,
    to_theirs_b,
    sum_own,
    sum_other,
    gscaled,
):
    wide = heads * BLOCK
    yh, z, core = meta[0], meta[1], meta[2]
    sum_own[...] = jnp.zeros(sum_own.shape, f32)
    sum_other[...] = jnp.zeros(sum_other.shape, f32)

    for w in range(2):
        log_sum, row_delta, log_top, filled = (stats[w, i : i + 1, :] for i in range(4))
        log_all, near, far = shares(log_sum, come[0:1, :], (1 - yh) == w)
        scale = jnp.where(filled > 0.0, jnp.exp2(log_top - log_all), 0.0)
        delta = (row_delta * near + come[1:2, :] * far) * scale
        gout = gout_t[w] * scale
        for h in range(heads):
            columns = slice(h * HEAD, (h + 1) * HEAD)
            gscaled[h * BLOCK : (h + 1) * BLOCK, :] = gout[:, columns].T.astype(bf16)
        grads = gscaled[...]
        queries = query[w]
        first_quad, last_quad = quad_range(meta, z_count, w, start_ref[w])

        def step(quad, dq):
            keys, dscores = [], []
            places = chip_pieces(core, (own, sum_own), (other, sum_other), quad)
            for n, ((src, dst), z_at, _) in enumerate(places):
                p = prob[w, quad, rows_of(n), :]
                dp = last_last(src[z_at, VALUES, :], grads)
                ds = (p.astype(f32) * (dp - delta)).astype(bf16)
                dst[z_at, KEYS, :] += plain(ds, queries)
                dst[z_at, VALUES, :] += plain(p, grads)
                keys.append(src[z_at, KEYS, :])
                dscores.append(ds)
            return dq + first_first(
                jnp.concatenate(keys, axis=0), jnp.concatenate(dscores, axis=0)
            )

        dq = lax.fori_loop(first_quad, last_quad + 1, step, jnp.zeros((HEAD, wide), f32))
        dq = dq * inverse
        low = low_ref[w]
        for h in range(heads):
            columns = slice(h * HEAD, (h + 1) * HEAD)
            dq_h = dq[:, columns].T
            dq_low = dq_h.astype(bf16)
            if w == 0:
                dquery[:, columns] = dq_h
            else:
                dquery_across[:, columns] = dq_low
            up = adapter_scale * first_first(low, dq_low)
            for j in range(2):
                z_at, slot = expert_at(meta, z_count, w, j)
                at = pl.ds(pl.multiple_of(KV + slot * UPS + 16 * h, 16), 16)
                for i in range(2):
                    row = j * RANK + 32 * i
                    even, odd = up[row : row + 16, :], up[row + 16 : row + 32, :]
                    sum_own[z_at + i, at, :] += jnp.where(core == 0, even, odd)
                    sum_other[z_at + i, at, :] += jnp.where(core == 0, odd, even)

    def put(first, second, at, src, z_at, valid):
        keep = jnp.where(valid, 1.0, 0.0)
        keys = (src[z_at, KEYS, :] * (inverse * keep)).astype(bf16)
        rest = (src[z_at, BLOCK:GRAD, :] * keep).astype(bf16)
        first[(*at, slice(0, BLOCK))] = keys
        first[(*at, slice(BLOCK, HALF))] = rest[0 : HALF - BLOCK]
        second[at] = rest[HALF - BLOCK :]

    steps = z_count // 2
    put(to_own_a, to_own_b, (0,), sum_own, z, True)
    put(to_own_a, to_own_b, (1,), sum_other, z, True)
    for d in range(steps):
        up, down = lax.rem(z + d + 1, z_count), lax.rem(z - d - 1 + z_count, z_count)
        here, there = jnp.where(core == 0, up, down), jnp.where(core == 0, down, up)
        inner = d < steps - 1
        for r, src in enumerate((sum_own, sum_other)):
            put(to_mine_a, to_mine_b, (d, r), src, here, inner or core == 0)
            put(to_theirs_a, to_theirs_b, (d, 1 - r), src, there, inner or core == 1)


def finish(heads, meta, out_t, stats, come, far_out, far_dquery, dquery, attended, dquery_out):
    _, near, far = shares(stats[0, 0:1, :], come[0:1, :], meta[0] == 1)
    out = out_t[0] * near + far_out[...].astype(f32) * far
    for h in range(heads):
        columns = slice(h * HEAD, (h + 1) * HEAD)
        attended[:, columns] = out[:, columns].T
    dquery_out[...] = dquery[...] + far_dquery[...].astype(f32)


def swap(array, distance):
    count = lax.axis_size("ctx")
    return lax.ppermute(array, "ctx", [(i, i ^ distance) for i in range(count)])


def pass_on(array):
    z_count = lax.axis_size("ctx") // 4
    route = []
    for yh in range(2):
        for z in range(z_count):
            for core in range(2):
                to = (z + (-1 if core else 1)) % z_count
                route.append(((yh * z_count + z) * 2 + core, (yh * z_count + to) * 2 + core))
    return lax.ppermute(array, "ctx", route)


def added(*parts):
    return sum(part.astype(f32) for part in parts).astype(bf16)


def shards(
    normed,
    frozen_query,
    input_keys,
    input_values,
    document_index,
    routes,
    adapter_down_weight,
    adapter_up_weight,
    output_gradient,
):
    z_count = lax.axis_size("ctx") // 4
    across = 2 * z_count
    exp_count = lax.axis_size("exp")
    place = lax.axis_index("ctx")
    steps = z_count // 2
    runs = [
        [(yh * z_count + z) * 2 + core for z in range(z_count)]
        for yh in range(2)
        for core in range(2)
    ]
    rows = normed.shape[0]
    wide = frozen_query.shape[1]
    heads = wide // HEAD
    stack = heads * rows
    up_rows = adapter_up_weight.shape[0]
    vmem = pl.BlockSpec(memory_space=pltpu.VMEM)
    smem = pl.BlockSpec(memory_space=pltpu.SMEM)

    ups = adapter_up_weight.reshape(up_rows, heads, HEAD).transpose(1, 0, 2)
    ups = ups.reshape(up_rows * heads, HEAD)
    lower = document_index[:, None] < jnp.arange(128, dtype=jnp.int32)[None, :]
    counts = jnp.sum(lower.astype(f32), axis=0, keepdims=True).astype(bf16)
    small = jnp.concatenate([ups, jnp.pad(counts, ((0, 15), (0, 0)))], axis=0)
    small_across = swap(small, across)
    pack = jnp.concatenate(
        [
            input_keys,
            input_values,
            ups,
            small_across[:UPS],
            small[UPS:] + small_across[UPS:],
        ],
        axis=0,
    )
    own = lax.all_gather(pack, "ctx", axis=0, tiled=False, axis_index_groups=runs)

    chosen = [
        lax.dynamic_index_in_dim(adapter_down_weight, routes[0, j], 0, keepdims=False)
        for j in range(2)
    ]
    partial = jnp.dot(normed, jnp.concatenate(chosen, axis=1), preferred_element_type=f32)
    lows = lax.all_to_all(
        jnp.broadcast_to(partial[None], (exp_count,) + partial.shape), "exp", 0, 0
    )
    low = pl.pallas_call(
        sum_low,
        out_shape=jax.ShapeDtypeStruct(partial.shape, bf16),
        in_specs=[vmem],
        out_specs=vmem,
    )(lows)
    low = jnp.stack([low, swap(low, across)])
    local = jnp.concatenate([frozen_query, output_gradient], axis=0)
    local, _ = lax.optimization_barrier((local, pack))
    pair = jnp.stack([local, swap(local, across)])
    ints = jnp.concatenate(
        [document_index.reshape(1, rows), jnp.pad(routes, ((0, 7 - 1), (0, rows - 2)))], axis=0
    )
    ints, _ = lax.optimization_barrier((ints, pack))
    ints = jnp.stack([ints, swap(ints, across)])
    frozen, gout_t, pick = pl.pallas_call(
        functools.partial(prepare, heads),
        out_shape=(
            jax.ShapeDtypeStruct((2, stack, HEAD), bf16),
            jax.ShapeDtypeStruct((2, HEAD, stack), f32),
            jax.ShapeDtypeStruct((2, 128, rows), bf16),
        ),
        in_specs=[vmem] * 2,
        out_specs=(vmem,) * 3,
    )(pair, ints)
    meta = jnp.stack(
        [
            place // across,
            place // 2 % z_count,
            place % 2,
            ints[0, 1, 0],
            ints[0, 1, 1],
            ints[1, 1, 0],
            ints[1, 1, 1],
        ]
    ).astype(jnp.int32)
    own, low, frozen, gout_t, pick, meta = lax.optimization_barrier(
        (own, low, frozen, gout_t, pick, meta)
    )
    other = swap(own, 1)

    quads = z_count // 2
    query, start, prob, out, stats = pl.pallas_call(
        functools.partial(forward, heads, z_count),
        out_shape=(
            jax.ShapeDtypeStruct((2, stack, HEAD), bf16),
            jax.ShapeDtypeStruct((2, 8, stack), jnp.int32),
            jax.ShapeDtypeStruct((2, quads, QUAD, stack), bf16),
            jax.ShapeDtypeStruct((2, HEAD, stack), f32),
            jax.ShapeDtypeStruct((2, 8, stack), f32),
        ),
        in_specs=[smem] + [vmem] * 6,
        out_specs=(vmem,) * 5,
        scratch_shapes=[pltpu.VMEM((quads, QUAD, stack), f32)],
        compiler_params=pltpu.CompilerParams(vmem_limit_bytes=30 * 1024 * 1024),
    )(meta, own, other, low, frozen, pick, gout_t)
    come = swap(jnp.where(place < across, stats[1], stats[0]), across)

    to_chip = jax.ShapeDtypeStruct((2, HALF, HEAD), bf16)
    to_chips = jax.ShapeDtypeStruct((steps, 2, HALF, HEAD), bf16)
    dquery, dquery_across, own_a, own_b, mine_a, mine_b, theirs_a, theirs_b = pl.pallas_call(
        functools.partial(backward, heads, z_count),
        out_shape=(
            jax.ShapeDtypeStruct((rows, wide), f32),
            jax.ShapeDtypeStruct((rows, wide), bf16),
            to_chip,
            to_chip,
            to_chips,
            to_chips,
            to_chips,
            to_chips,
        ),
        in_specs=[smem] + [vmem] * 9,
        out_specs=(vmem,) * 8,
        scratch_shapes=[
            pltpu.VMEM((z_count, GRAD, HEAD), f32),
            pltpu.VMEM((z_count, GRAD, HEAD), f32),
            pltpu.VMEM((stack, HEAD), bf16),
        ],
        compiler_params=pltpu.CompilerParams(vmem_limit_bytes=30 * 1024 * 1024),
    )(meta, own, other, query, start, prob, stats, come, gout_t, low)

    from_a, from_b = swap(theirs_a, 1), swap(theirs_b, 1)
    sum_a = added(mine_a[steps - 1], from_a[steps - 1])
    sum_b = added(mine_b[steps - 1], from_b[steps - 1])
    first_sum = sum_a
    for d in reversed(range(steps)):
        sum_a, sum_b = pass_on(sum_a), pass_on(sum_b)
        if d > 0:
            sum_a = added(sum_a, mine_a[d - 1], from_a[d - 1])
            sum_b = added(sum_b, mine_b[d - 1], from_b[d - 1])
    part = jnp.concatenate([added(sum_a, own_a), added(sum_b, own_b)], axis=1)

    far_out = jnp.where(place < across, out[1], out[0]).astype(bf16)
    far, _ = lax.optimization_barrier((jnp.stack([far_out, dquery_across.reshape(HEAD, stack)]), first_sum))
    far = swap(far, across)
    attended, dquery = pl.pallas_call(
        functools.partial(finish, heads),
        out_shape=(jax.ShapeDtypeStruct((rows, wide), f32),) * 2,
        in_specs=[smem] + [vmem] * 6,
        out_specs=(vmem,) * 2,
    )(meta, out, stats, come, far[0], far[1].reshape(rows, wide), dquery)

    main = slice(0, KV + UPS)
    grads = part[0, main].astype(f32) + swap(part[1, main], 1).astype(f32)
    up_grad = (
        grads[KV:]
        + swap(part[0, KV + UPS :], across).astype(f32)
        + swap(part[1, KV + UPS :], across ^ 1).astype(f32)
    )
    up_grad = up_grad.reshape(heads, up_rows, HEAD).transpose(1, 0, 2)
    return (
        attended,
        dquery,
        grads[KEYS],
        grads[VALUES],
        up_grad.reshape(up_rows, wide),
    )


def solution(mesh):
    both = P("ctx", "exp")
    return jax.shard_map(
        shards,
        mesh=mesh,
        in_specs=(
            both,
            both,
            both,
            both,
            P("ctx"),
            P("ctx", None),
            P(None, "exp", None),
            both,
            both,
        ),
        out_specs=(both,) * 5,
        check_vma=False,
    )
```

```python
import functools
import math

import jax
import jax.numpy as jnp
from jax import lax
from jax.experimental import pallas as pl
from jax.experimental.pallas import tpu as pltpu
from jax.sharding import PartitionSpec as P

HEAD = 128
RANK = 64
BLOCK = 128
QUAD = 4 * BLOCK

adapter_scale = 0.5
far_below = -1e30
to_two = math.log2(math.e) / math.sqrt(HEAD)
inverse = 1.0 / math.sqrt(HEAD)
f32 = jnp.float32
bf16 = jnp.bfloat16

KV = 2 * BLOCK
UPS = 64
GRAD = KV + 2 * UPS
SMALL = UPS + 16

STACK = 4 * BLOCK
GOUT_AT, LOW_AT, START_AT = STACK, 2 * STACK, 2 * STACK + BLOCK
SIDE = START_AT + 16
KEYS, VALUES = slice(0, BLOCK), slice(BLOCK, KV)


def last_last(a, b):
    return lax.dot_general(a, b, (((1,), (1,)), ((), ())), preferred_element_type=f32)


def first_first(a, b):
    return lax.dot_general(a, b, (((0,), (0,)), ((), ())), preferred_element_type=f32)


def plain(a, b):
    return lax.dot_general(a, b, (((1,), (0,)), ((), ())), preferred_element_type=f32)


def sum_low(lows, low_out):
    low = lows[0]
    for i in range(1, lows.shape[0]):
        low = low + lows[i]
    low_out[...] = low.astype(bf16)


def expert_at(meta, z_count, w, j):
    first = meta[3 + 2 * w + j] * 4
    return lax.rem(first, 2 * z_count) // 2, lax.div(first, 2 * z_count) ^ meta[0]


def query_base(meta, z_count, w):
    yh, z, core = meta[0], meta[1], meta[2]
    across = (1 - 2 * yh) * 2 * z_count * BLOCK
    return (2 * z + core) * BLOCK + w * across


def quad_range(meta, z_count, w, start):
    base = query_base(meta, z_count, w)
    first_key = jnp.min(start.astype(f32)).astype(jnp.int32)
    first = jnp.clip(first_key, 0, z_count * KV) // QUAD
    last = jnp.clip(base, -QUAD, z_count * KV - 1) // QUAD
    last = jnp.where(base < 0, -1, last)
    return first, last


def prepare(heads, z_count, meta, own, other, low_ref, pair, docs, side):
    core = meta[2]

    counts = jnp.zeros((16, 128), f32)
    for i in range(z_count):
        for slot in range(2):
            for ref in (own, other):
                counts += ref[slot, i, UPS:SMALL, :].astype(f32)
    high = jnp.floor(counts * (1.0 / 128.0))
    rest = (counts - 128.0 * high).astype(bf16)
    high = high.astype(bf16)
    lane = lax.broadcasted_iota(jnp.int32, (128, BLOCK), 0)

    for w in range(2):
        low = low_ref[w]
        side[w, LOW_AT:START_AT, :] = low
        for h in range(heads):
            columns = slice(h * HEAD, (h + 1) * HEAD)
            rows = []
            for j in range(2):
                z_at, slot = expert_at(meta, z_count, w, j)
                at = slice(16 * h, 16 * h + 16)
                for step in range(2):
                    mine, theirs = own[slot, z_at + step, at, :], other[slot, z_at + step, at, :]
                    rows.append(jnp.where(core == 0, mine, theirs))
                    rows.append(jnp.where(core == 0, theirs, mine))
            delta = plain(low, jnp.concatenate(rows, axis=0))
            side[w, h * BLOCK : (h + 1) * BLOCK, :] = (
                pair[w, 0:BLOCK, columns].astype(f32) + adapter_scale * delta
            ).astype(bf16)
            gout = pair[w, BLOCK : 2 * BLOCK, columns].astype(f32).T
            side[w, GOUT_AT + h * HEAD : GOUT_AT + (h + 1) * HEAD, :] = gout.astype(bf16)
        pick = jnp.where(lane == docs[w, 0:1, :], 1.0, 0.0).astype(bf16)
        whole = jnp.sum(plain(high, pick), axis=0, keepdims=True)
        part = jnp.sum(plain(rest, pick), axis=0, keepdims=True)
        side[w, START_AT:SIDE, :] = jnp.concatenate(
            [whole, part, jnp.zeros((14, BLOCK), f32)], axis=0
        ).astype(bf16)


def stage(own, side, own_out, side_out):
    own_out[...] = own[...]
    side_out[...] = side[...]


def start_of(meta, z_count, side, w):
    rows = side[w, START_AT:SIDE, :].astype(f32)
    start = 128.0 * rows[0:1] + rows[1:2]
    return start.astype(jnp.int32) - meta[0] * (z_count * KV)


def gout_of(heads, side, w):
    blocks = [side[w, GOUT_AT + h * HEAD : GOUT_AT + (h + 1) * HEAD, :] for h in range(heads)]
    return jnp.concatenate(blocks, axis=1).astype(f32)


def chip_pieces(core, own, other, quad):
    z_at = quad * 2
    return [
        (own, z_at, core),
        (other, z_at, 1 - core),
        (own, z_at + 1, 2 + core),
        (other, z_at + 1, 3 - core),
    ]


def rows_of(n):
    return slice(n * BLOCK, (n + 1) * BLOCK)


def forward(heads, z_count, meta, own, other, side, prob, out_ref, stats, score):
    wide = heads * BLOCK
    core = meta[2]
    ramp = lax.broadcasted_iota(jnp.int32, (BLOCK, wide), 0)

    for w in range(2):
        start = start_of(meta, z_count, side, w)
        whole_key = jnp.max(start.astype(f32)).astype(jnp.int32)
        first_quad, last_quad = quad_range(meta, z_count, w, start)
        start = jnp.concatenate([start] * heads, axis=1)
        place = query_base(meta, z_count, w) + lax.broadcasted_iota(jnp.int32, (1, BLOCK), 1)
        place = jnp.concatenate([place] * heads, axis=1)
        whole_key = jnp.clip(whole_key, 0, z_count * KV)
        whole_quad = jnp.minimum(
            jnp.maximum((whole_key + QUAD - 1) // QUAD, first_quad), last_quad
        )
        queries = side[w, 0:STACK, :]

        def scores(masked, quad, top):
            for n, (src, z_at, at) in enumerate(chip_pieces(core, own, other, quad)):
                s = last_last(src[z_at, KEYS, :], queries)
                if masked:
                    base = quad * QUAD + at * BLOCK
                    s = jnp.where((ramp >= start - base) & (ramp <= place - base), s, far_below)
                score[quad, rows_of(n), :] = s
                top = jnp.maximum(top, jnp.max(s.reshape(BLOCK // 8, 8, wide), axis=0))
            return top

        top = jnp.full((8, wide), far_below, f32)
        top = lax.fori_loop(
            first_quad,
            jnp.where(last_quad >= first_quad, whole_quad + 1, first_quad),
            lambda i, t: scores(True, jnp.where(i == whole_quad, last_quad, i), t),
            top,
        )
        top = lax.fori_loop(
            jnp.maximum(whole_quad, first_quad),
            last_quad,
            functools.partial(scores, False),
            top,
        )
        top = jnp.max(top, axis=0, keepdims=True)
        top = jnp.where(top < 0.5 * far_below, 0.0, top)

        def attend(quad, carry):
            total, out = carry
            values = []
            for n, (src, z_at, _) in enumerate(chip_pieces(core, own, other, quad)):
                p = jnp.exp2((score[quad, rows_of(n), :] - top) * to_two)
                total = total + jnp.sum(p.reshape(BLOCK // 8, 8, wide), axis=0)
                prob[w, quad, rows_of(n), :] = p.astype(bf16)
                values.append(src[z_at, VALUES, :])
            out = out + first_first(jnp.concatenate(values, axis=0), prob[w, quad])
            return total, out

        total, out = lax.fori_loop(
            first_quad,
            last_quad + 1,
            attend,
            (jnp.zeros((8, wide), f32), jnp.zeros((HEAD, wide), f32)),
        )
        total = jnp.sum(total, axis=0, keepdims=True)
        some = total > 0.0
        safe = jnp.where(some, total, 1.0)
        out = out * (1.0 / safe)
        out_ref[w] = out
        row_delta = jnp.sum(gout_of(heads, side, w) * out, axis=0, keepdims=True)
        log_top = top * to_two
        log_sum = jnp.where(some, log_top + jnp.log2(safe), far_below)
        filled = jnp.where(some, 1.0, 0.0)
        stats[w] = jnp.concatenate(
            [log_sum, row_delta, log_top, filled, jnp.zeros((4, wide), f32)], axis=0
        )


def shares(log_sum, far_log, crossed):
    far_log = jnp.where(crossed, far_log, far_below)
    most = jnp.maximum(log_sum, far_log)
    log_all = most + jnp.log2(jnp.exp2(log_sum - most) + jnp.exp2(far_log - most))
    far = jnp.where(crossed, jnp.exp2(far_log - log_all), 0.0)
    return log_all, jnp.exp2(log_sum - log_all), far


def backward(
    heads,
    z_count,
    meta,
    own,
    other,
    side,
    prob,
    stats,
    come,
    dquery,
    dquery_across,
    send_own,
    send_other,
    sum_own,
    sum_other,
    gscaled,
):
    wide = heads * BLOCK
    yh, core = meta[0], meta[2]
    sum_own[...] = jnp.zeros(sum_own.shape, f32)
    sum_other[...] = jnp.zeros(sum_other.shape, f32)

    for w in range(2):
        log_sum, row_delta, log_top, filled = (stats[w, i : i + 1, :] for i in range(4))
        log_all, near, far = shares(log_sum, come[0:1, :], (1 - yh) == w)
        scale = jnp.where(filled > 0.0, jnp.exp2(log_top - log_all), 0.0)
        delta = (row_delta * near + come[1:2, :] * far) * scale
        gout = gout_of(heads, side, w) * scale
        for h in range(heads):
            columns = slice(h * HEAD, (h + 1) * HEAD)
            gscaled[h * BLOCK : (h + 1) * BLOCK, :] = gout[:, columns].T.astype(bf16)
        grads = gscaled[...]
        queries = side[w, 0:STACK, :]
        first_quad, last_quad = quad_range(
            meta, z_count, w, start_of(meta, z_count, side, w)
        )

        def step(quad, dq):
            keys, dscores = [], []
            places = chip_pieces(core, (own, sum_own), (other, sum_other), quad)
            for n, ((src, dst), z_at, _) in enumerate(places):
                p = prob[w, quad, rows_of(n), :]
                dp = last_last(src[z_at, VALUES, :], grads)
                ds = (p.astype(f32) * (dp - delta)).astype(bf16)
                dst[z_at, KEYS, :] += plain(ds, queries)
                dst[z_at, VALUES, :] += plain(p, grads)
                keys.append(src[z_at, KEYS, :])
                dscores.append(ds)
            return dq + first_first(
                jnp.concatenate(keys, axis=0), jnp.concatenate(dscores, axis=0)
            )

        dq = lax.fori_loop(first_quad, last_quad + 1, step, jnp.zeros((HEAD, wide), f32))
        dq = dq * inverse
        low = side[w, LOW_AT:START_AT, :]
        for h in range(heads):
            columns = slice(h * HEAD, (h + 1) * HEAD)
            dq_h = dq[:, columns].T
            dq_low = dq_h.astype(bf16)
            if w == 0:
                dquery[:, columns] = dq_h
            else:
                dquery_across[:, columns] = dq_low
            up = adapter_scale * first_first(low, dq_low)
            for j in range(2):
                z_at, slot = expert_at(meta, z_count, w, j)
                at = pl.ds(pl.multiple_of(KV + slot * UPS + 16 * h, 16), 16)
                for i in range(2):
                    row = j * RANK + 32 * i
                    even, odd = up[row : row + 16, :], up[row + 16 : row + 32, :]
                    sum_own[z_at + i, at, :] += jnp.where(core == 0, even, odd)
                    sum_other[z_at + i, at, :] += jnp.where(core == 0, odd, even)

    for src, dst in ((sum_own, send_own), (sum_other, send_other)):
        dst[:, KEYS, :] = (src[:, KEYS, :] * inverse).astype(bf16)
        dst[:, BLOCK:GRAD, :] = src[:, BLOCK:GRAD, :].astype(bf16)


def finish(heads, meta, out_t, stats, come, far_out, far_dquery, dquery, attended, dquery_out):
    _, near, far = shares(stats[0, 0:1, :], come[0:1, :], meta[0] == 1)
    out = out_t[0] * near + far_out[...].astype(f32) * far
    for h in range(heads):
        columns = slice(h * HEAD, (h + 1) * HEAD)
        attended[:, columns] = out[:, columns].T
    dquery_out[...] = dquery[...] + far_dquery[...].astype(f32)


def swap(array, distance):
    count = lax.axis_size("ctx")
    return lax.ppermute(array, "ctx", [(i, i ^ distance) for i in range(count)])


def shards(
    normed,
    frozen_query,
    input_keys,
    input_values,
    document_index,
    routes,
    adapter_down_weight,
    adapter_up_weight,
    output_gradient,
):
    z_count = lax.axis_size("ctx") // 4
    across = 2 * z_count
    exp_count = lax.axis_size("exp")
    place = lax.axis_index("ctx")
    runs = [
        [(yh * z_count + z) * 2 + core for z in range(z_count)]
        for yh in range(2)
        for core in range(2)
    ]
    rows = normed.shape[0]
    wide = frozen_query.shape[1]
    heads = wide // HEAD
    stack = heads * rows
    up_rows = adapter_up_weight.shape[0]
    vmem = pl.BlockSpec(memory_space=pltpu.VMEM)
    smem = pl.BlockSpec(memory_space=pltpu.SMEM)

    kv = jnp.concatenate([input_keys, input_values], axis=0)
    own = lax.all_gather(kv, "ctx", axis=0, tiled=False, axis_index_groups=runs)

    ups = adapter_up_weight.reshape(up_rows, heads, HEAD).transpose(1, 0, 2)
    ups = ups.reshape(up_rows * heads, HEAD)
    lower = document_index[:, None] < jnp.arange(128, dtype=jnp.int32)[None, :]
    counts = jnp.sum(lower.astype(f32), axis=0, keepdims=True).astype(bf16)
    small = jnp.concatenate([ups, jnp.pad(counts, ((0, 15), (0, 0)))], axis=0)
    small, _ = lax.optimization_barrier((small, kv))
    small = lax.all_gather(small, "ctx", axis=0, tiled=False, axis_index_groups=runs)
    small = jnp.stack([small, swap(small, across)])
    small_other = swap(small, 1)

    chosen = [
        lax.dynamic_index_in_dim(adapter_down_weight, routes[0, j], 0, keepdims=False)
        for j in range(2)
    ]
    partial = jnp.dot(normed, jnp.concatenate(chosen, axis=1), preferred_element_type=f32)
    lows = lax.all_to_all(
        jnp.broadcast_to(partial[None], (exp_count,) + partial.shape), "exp", 0, 0
    )
    low = pl.pallas_call(
        sum_low,
        out_shape=jax.ShapeDtypeStruct(partial.shape, bf16),
        in_specs=[vmem],
        out_specs=vmem,
    )(lows)
    low = jnp.stack([low, swap(low, across)])
    local = jnp.concatenate([frozen_query, output_gradient], axis=0)
    local, _ = lax.optimization_barrier((local, kv))
    pair = jnp.stack([local, swap(local, across)])
    ints = jnp.concatenate(
        [document_index.reshape(1, rows), jnp.pad(routes, ((0, 7 - 1), (0, rows - 2)))], axis=0
    )
    ints, _ = lax.optimization_barrier((ints, kv))
    ints = jnp.stack([ints, swap(ints, across)])
    meta = jnp.stack(
        [
            place // across,
            place // 2 % z_count,
            place % 2,
            ints[0, 1, 0],
            ints[0, 1, 1],
            ints[1, 1, 0],
            ints[1, 1, 1],
        ]
    ).astype(jnp.int32)
    side = pl.pallas_call(
        functools.partial(prepare, heads, z_count),
        out_shape=jax.ShapeDtypeStruct((2, SIDE, HEAD), bf16),
        in_specs=[smem] + [vmem] * 5,
        out_specs=vmem,
    )(meta, small, small_other, low, pair, ints)
    own, side = lax.optimization_barrier((own, side))
    other = swap(own, 1)
    own, side = pl.pallas_call(
        stage,
        out_shape=(
            jax.ShapeDtypeStruct(own.shape, bf16),
            jax.ShapeDtypeStruct(side.shape, bf16),
        ),
        in_specs=[vmem] * 2,
        out_specs=(vmem,) * 2,
    )(own, side)

    quads = z_count // 2
    prob, out, stats = pl.pallas_call(
        functools.partial(forward, heads, z_count),
        out_shape=(
            jax.ShapeDtypeStruct((2, quads, QUAD, stack), bf16),
            jax.ShapeDtypeStruct((2, HEAD, stack), f32),
            jax.ShapeDtypeStruct((2, 8, stack), f32),
        ),
        in_specs=[smem] + [vmem] * 3,
        out_specs=(vmem,) * 3,
        scratch_shapes=[pltpu.VMEM((quads, QUAD, stack), f32)],
        compiler_params=pltpu.CompilerParams(vmem_limit_bytes=30 * 1024 * 1024),
    )(meta, own, other, side)
    come = swap(jnp.where(place < across, stats[1], stats[0]), across)

    send = jax.ShapeDtypeStruct((z_count, GRAD, HEAD), bf16)
    dquery, dquery_across, send_own, send_other = pl.pallas_call(
        functools.partial(backward, heads, z_count),
        out_shape=(
            jax.ShapeDtypeStruct((rows, wide), f32),
            jax.ShapeDtypeStruct((rows, wide), bf16),
            send,
            send,
        ),
        in_specs=[smem] + [vmem] * 6,
        out_specs=(vmem,) * 4,
        scratch_shapes=[
            pltpu.VMEM((z_count, GRAD, HEAD), f32),
            pltpu.VMEM((z_count, GRAD, HEAD), f32),
            pltpu.VMEM((stack, HEAD), bf16),
        ],
        compiler_params=pltpu.CompilerParams(vmem_limit_bytes=30 * 1024 * 1024),
    )(meta, own, other, side, prob, stats, come)

    chip = send_own + swap(send_other, 1)
    part = lax.psum_scatter(
        chip, "ctx", scatter_dimension=0, tiled=False, axis_index_groups=runs
    )

    far_out = jnp.where(place < across, out[1], out[0]).astype(bf16)
    far, _ = lax.optimization_barrier((jnp.stack([far_out, dquery_across.reshape(HEAD, stack)]), chip))
    far = swap(far, across)
    attended, dquery = pl.pallas_call(
        functools.partial(finish, heads),
        out_shape=(jax.ShapeDtypeStruct((rows, wide), f32),) * 2,
        in_specs=[smem] + [vmem] * 6,
        out_specs=(vmem,) * 2,
    )(meta, out, stats, come, far[0], far[1].reshape(rows, wide), dquery)

    up_grad = part[KV : KV + UPS].astype(f32) + swap(part[KV + UPS :], across).astype(f32)
    up_grad = up_grad.reshape(heads, up_rows, HEAD).transpose(1, 0, 2)
    return (
        attended,
        dquery,
        part[KEYS].astype(f32),
        part[VALUES].astype(f32),
        up_grad.reshape(up_rows, wide),
    )


def solution(mesh):
    both = P("ctx", "exp")
    return jax.shard_map(
        shards,
        mesh=mesh,
        in_specs=(
            both,
            both,
            both,
            both,
            P("ctx"),
            P("ctx", None),
            P(None, "exp", None),
            both,
            both,
        ),
        out_specs=(both,) * 5,
        check_vma=False,
    )
```

```python
import functools
import math

import jax
import jax.numpy as jnp
from jax import lax
from jax.experimental import pallas as pl
from jax.experimental.pallas import tpu as pltpu
from jax.sharding import PartitionSpec as P

HEAD = 128
RANK = 64
BLOCK = 128
QUAD = 4 * BLOCK

adapter_scale = 0.5
far_below = -1e30
to_two = math.log2(math.e) / math.sqrt(HEAD)
inverse = 1.0 / math.sqrt(HEAD)
f32 = jnp.float32
bf16 = jnp.bfloat16

KV = 2 * BLOCK
UPS = 64
GRAD = KV + 2 * UPS
SMALL = UPS + 16

STACK = 4 * BLOCK
GOUT_AT, LOW_AT, START_AT = STACK, 2 * STACK, 2 * STACK + BLOCK
SIDE = START_AT + 16
KEYS, VALUES = slice(0, BLOCK), slice(BLOCK, KV)


def last_last(a, b):
    return lax.dot_general(a, b, (((1,), (1,)), ((), ())), preferred_element_type=f32)


def first_first(a, b):
    return lax.dot_general(a, b, (((0,), (0,)), ((), ())), preferred_element_type=f32)


def plain(a, b):
    return lax.dot_general(a, b, (((1,), (0,)), ((), ())), preferred_element_type=f32)


def sum_low(lows, low_out):
    low = lows[0]
    for i in range(1, lows.shape[0]):
        low = low + lows[i]
    low_out[...] = low.astype(bf16)


def expert_at(meta, z_count, w, j):
    first = meta[3 + 2 * w + j] * 4
    return lax.rem(first, 2 * z_count) // 2, lax.div(first, 2 * z_count) ^ meta[0]


def query_base(meta, z_count, w):
    yh, z, core = meta[0], meta[1], meta[2]
    across = (1 - 2 * yh) * 2 * z_count * BLOCK
    return (2 * z + core) * BLOCK + w * across


def quad_range(meta, z_count, w, start):
    base = query_base(meta, z_count, w)
    first_key = jnp.min(start.astype(f32)).astype(jnp.int32)
    first = jnp.clip(first_key, 0, z_count * KV) // QUAD
    last = jnp.clip(base, -QUAD, z_count * KV - 1) // QUAD
    last = jnp.where(base < 0, -1, last)
    return first, last


def prepare(heads, z_count, meta, own, other, low_ref, pair, docs, side):
    core = meta[2]

    counts = jnp.zeros((16, 128), f32)
    for i in range(z_count):
        for slot in range(2):
            for ref in (own, other):
                counts += ref[slot, i, UPS:SMALL, :].astype(f32)
    high = jnp.floor(counts * (1.0 / 128.0))
    rest = (counts - 128.0 * high).astype(bf16)
    high = high.astype(bf16)
    lane = lax.broadcasted_iota(jnp.int32, (128, BLOCK), 0)

    for w in range(2):
        low = low_ref[w]
        side[w, LOW_AT:START_AT, :] = low
        for h in range(heads):
            columns = slice(h * HEAD, (h + 1) * HEAD)
            rows = []
            for j in range(2):
                z_at, slot = expert_at(meta, z_count, w, j)
                at = slice(16 * h, 16 * h + 16)
                for step in range(2):
                    mine, theirs = own[slot, z_at + step, at, :], other[slot, z_at + step, at, :]
                    rows.append(jnp.where(core == 0, mine, theirs))
                    rows.append(jnp.where(core == 0, theirs, mine))
            delta = plain(low, jnp.concatenate(rows, axis=0))
            side[w, h * BLOCK : (h + 1) * BLOCK, :] = (
                pair[w, 0:BLOCK, columns].astype(f32) + adapter_scale * delta
            ).astype(bf16)
            gout = pair[w, BLOCK : 2 * BLOCK, columns].astype(f32).T
            side[w, GOUT_AT + h * HEAD : GOUT_AT + (h + 1) * HEAD, :] = gout.astype(bf16)
        pick = jnp.where(lane == docs[w, 0:1, :], 1.0, 0.0).astype(bf16)
        whole = jnp.sum(plain(high, pick), axis=0, keepdims=True)
        part = jnp.sum(plain(rest, pick), axis=0, keepdims=True)
        side[w, START_AT:SIDE, :] = jnp.concatenate(
            [whole, part, jnp.zeros((14, BLOCK), f32)], axis=0
        ).astype(bf16)


def start_of(meta, z_count, side, w):
    rows = side[w, START_AT:SIDE, :].astype(f32)
    start = 128.0 * rows[0:1] + rows[1:2]
    return start.astype(jnp.int32) - meta[0] * (z_count * KV)


def gout_of(heads, side, w):
    blocks = [side[w, GOUT_AT + h * HEAD : GOUT_AT + (h + 1) * HEAD, :] for h in range(heads)]
    return jnp.concatenate(blocks, axis=1).astype(f32)


def chip_pieces(core, own, other, quad):
    z_at = quad * 2
    return [
        (own, z_at, core),
        (other, z_at, 1 - core),
        (own, z_at + 1, 2 + core),
        (other, z_at + 1, 3 - core),
    ]


def rows_of(n):
    return slice(n * BLOCK, (n + 1) * BLOCK)


def forward(heads, z_count, meta, own, other, side, prob, out_ref, stats, score):
    wide = heads * BLOCK
    core = meta[2]
    ramp = lax.broadcasted_iota(jnp.int32, (BLOCK, wide), 0)

    for w in range(2):
        start = start_of(meta, z_count, side, w)
        whole_key = jnp.max(start.astype(f32)).astype(jnp.int32)
        first_quad, last_quad = quad_range(meta, z_count, w, start)
        start = jnp.concatenate([start] * heads, axis=1)
        place = query_base(meta, z_count, w) + lax.broadcasted_iota(jnp.int32, (1, BLOCK), 1)
        place = jnp.concatenate([place] * heads, axis=1)
        whole_key = jnp.clip(whole_key, 0, z_count * KV)
        whole_quad = jnp.minimum(
            jnp.maximum((whole_key + QUAD - 1) // QUAD, first_quad), last_quad
        )
        queries = side[w, 0:STACK, :]

        def scores(masked, quad, top):
            for n, (src, z_at, at) in enumerate(chip_pieces(core, own, other, quad)):
                s = last_last(src[z_at, KEYS, :], queries)
                if masked:
                    base = quad * QUAD + at * BLOCK
                    s = jnp.where((ramp >= start - base) & (ramp <= place - base), s, far_below)
                score[quad, rows_of(n), :] = s
                top = jnp.maximum(top, jnp.max(s.reshape(BLOCK // 8, 8, wide), axis=0))
            return top

        top = jnp.full((8, wide), far_below, f32)
        top = lax.fori_loop(
            first_quad,
            jnp.where(last_quad >= first_quad, whole_quad + 1, first_quad),
            lambda i, t: scores(True, jnp.where(i == whole_quad, last_quad, i), t),
            top,
        )
        top = lax.fori_loop(
            jnp.maximum(whole_quad, first_quad),
            last_quad,
            functools.partial(scores, False),
            top,
        )
        top = jnp.max(top, axis=0, keepdims=True)
        top = jnp.where(top < 0.5 * far_below, 0.0, top)

        def attend(quad, carry):
            total, out = carry
            values = []
            for n, (src, z_at, _) in enumerate(chip_pieces(core, own, other, quad)):
                p = jnp.exp2((score[quad, rows_of(n), :] - top) * to_two)
                total = total + jnp.sum(p.reshape(BLOCK // 8, 8, wide), axis=0)
                prob[w, quad, rows_of(n), :] = p.astype(bf16)
                values.append(src[z_at, VALUES, :])
            out = out + first_first(jnp.concatenate(values, axis=0), prob[w, quad])
            return total, out

        total, out = lax.fori_loop(
            first_quad,
            last_quad + 1,
            attend,
            (jnp.zeros((8, wide), f32), jnp.zeros((HEAD, wide), f32)),
        )
        total = jnp.sum(total, axis=0, keepdims=True)
        some = total > 0.0
        safe = jnp.where(some, total, 1.0)
        out = out * (1.0 / safe)
        out_ref[w] = out
        row_delta = jnp.sum(gout_of(heads, side, w) * out, axis=0, keepdims=True)
        log_top = top * to_two
        log_sum = jnp.where(some, log_top + jnp.log2(safe), far_below)
        filled = jnp.where(some, 1.0, 0.0)
        stats[w] = jnp.concatenate(
            [log_sum, row_delta, log_top, filled, jnp.zeros((4, wide), f32)], axis=0
        )


def shares(log_sum, far_log, crossed):
    far_log = jnp.where(crossed, far_log, far_below)
    most = jnp.maximum(log_sum, far_log)
    log_all = most + jnp.log2(jnp.exp2(log_sum - most) + jnp.exp2(far_log - most))
    far = jnp.where(crossed, jnp.exp2(far_log - log_all), 0.0)
    return log_all, jnp.exp2(log_sum - log_all), far


def backward(
    heads,
    z_count,
    meta,
    own,
    other,
    side,
    prob,
    stats,
    come,
    dquery,
    dquery_across,
    send_own,
    send_other,
    sum_own,
    sum_other,
    gscaled,
):
    wide = heads * BLOCK
    yh, core = meta[0], meta[2]
    sum_own[...] = jnp.zeros(sum_own.shape, f32)
    sum_other[...] = jnp.zeros(sum_other.shape, f32)

    for w in range(2):
        log_sum, row_delta, log_top, filled = (stats[w, i : i + 1, :] for i in range(4))
        log_all, near, far = shares(log_sum, come[0:1, :], (1 - yh) == w)
        scale = jnp.where(filled > 0.0, jnp.exp2(log_top - log_all), 0.0)
        delta = (row_delta * near + come[1:2, :] * far) * scale
        gout = gout_of(heads, side, w) * scale
        for h in range(heads):
            columns = slice(h * HEAD, (h + 1) * HEAD)
            gscaled[h * BLOCK : (h + 1) * BLOCK, :] = gout[:, columns].T.astype(bf16)
        grads = gscaled[...]
        queries = side[w, 0:STACK, :]
        first_quad, last_quad = quad_range(
            meta, z_count, w, start_of(meta, z_count, side, w)
        )

        def step(quad, dq):
            keys, dscores = [], []
            places = chip_pieces(core, (own, sum_own), (other, sum_other), quad)
            for n, ((src, dst), z_at, _) in enumerate(places):
                p = prob[w, quad, rows_of(n), :]
                dp = last_last(src[z_at, VALUES, :], grads)
                ds = (p.astype(f32) * (dp - delta)).astype(bf16)
                dst[z_at, KEYS, :] += plain(ds, queries)
                dst[z_at, VALUES, :] += plain(p, grads)
                keys.append(src[z_at, KEYS, :])
                dscores.append(ds)
            return dq + first_first(
                jnp.concatenate(keys, axis=0), jnp.concatenate(dscores, axis=0)
            )

        dq = lax.fori_loop(first_quad, last_quad + 1, step, jnp.zeros((HEAD, wide), f32))
        dq = dq * inverse
        low = side[w, LOW_AT:START_AT, :]
        for h in range(heads):
            columns = slice(h * HEAD, (h + 1) * HEAD)
            dq_h = dq[:, columns].T
            dq_low = dq_h.astype(bf16)
            if w == 0:
                dquery[:, columns] = dq_h
            else:
                dquery_across[:, columns] = dq_low
            up = adapter_scale * first_first(low, dq_low)
            for j in range(2):
                z_at, slot = expert_at(meta, z_count, w, j)
                at = pl.ds(pl.multiple_of(KV + slot * UPS + 16 * h, 16), 16)
                for i in range(2):
                    row = j * RANK + 32 * i
                    even, odd = up[row : row + 16, :], up[row + 16 : row + 32, :]
                    sum_own[z_at + i, at, :] += jnp.where(core == 0, even, odd)
                    sum_other[z_at + i, at, :] += jnp.where(core == 0, odd, even)

    for src, dst in ((sum_own, send_own), (sum_other, send_other)):
        dst[:, KEYS, :] = (src[:, KEYS, :] * inverse).astype(bf16)
        dst[:, BLOCK:GRAD, :] = src[:, BLOCK:GRAD, :].astype(bf16)


def finish(heads, meta, out_t, stats, come, far_out, far_dquery, dquery, attended, dquery_out):
    _, near, far = shares(stats[0, 0:1, :], come[0:1, :], meta[0] == 1)
    out = out_t[0] * near + far_out[...].astype(f32) * far
    for h in range(heads):
        columns = slice(h * HEAD, (h + 1) * HEAD)
        attended[:, columns] = out[:, columns].T
    dquery_out[...] = dquery[...] + far_dquery[...].astype(f32)


def swap(array, distance):
    count = lax.axis_size("ctx")
    return lax.ppermute(array, "ctx", [(i, i ^ distance) for i in range(count)])


def shards(
    normed,
    frozen_query,
    input_keys,
    input_values,
    document_index,
    routes,
    adapter_down_weight,
    adapter_up_weight,
    output_gradient,
):
    z_count = lax.axis_size("ctx") // 4
    across = 2 * z_count
    exp_count = lax.axis_size("exp")
    place = lax.axis_index("ctx")
    runs = [
        [(yh * z_count + z) * 2 + core for z in range(z_count)]
        for yh in range(2)
        for core in range(2)
    ]
    rows = normed.shape[0]
    wide = frozen_query.shape[1]
    heads = wide // HEAD
    stack = heads * rows
    up_rows = adapter_up_weight.shape[0]
    vmem = pl.BlockSpec(memory_space=pltpu.VMEM)
    smem = pl.BlockSpec(memory_space=pltpu.SMEM)

    kv = jnp.concatenate([input_keys, input_values], axis=0)
    own = lax.all_gather(kv, "ctx", axis=0, tiled=False, axis_index_groups=runs)

    chosen = [
        lax.dynamic_index_in_dim(adapter_down_weight, routes[0, j], 0, keepdims=False)
        for j in range(2)
    ]
    partial = jnp.dot(normed, jnp.concatenate(chosen, axis=1), preferred_element_type=f32)
    spread = jnp.broadcast_to(partial[None], (exp_count,) + partial.shape)
    lows = lax.all_to_all(spread, "exp", 0, 0)
    low = pl.pallas_call(
        sum_low,
        out_shape=jax.ShapeDtypeStruct(partial.shape, bf16),
        in_specs=[vmem],
        out_specs=vmem,
    )(lows)
    ups = adapter_up_weight.reshape(up_rows, heads, HEAD).transpose(1, 0, 2)
    ups = ups.reshape(up_rows * heads, HEAD)
    lower = document_index[:, None] < jnp.arange(128, dtype=jnp.int32)[None, :]
    counts = jnp.sum(lower.astype(f32), axis=0, keepdims=True).astype(bf16)
    small = jnp.concatenate([ups, jnp.pad(counts, ((0, 15), (0, 0)))], axis=0)
    small, _ = lax.optimization_barrier((small, (kv, spread)))
    small = lax.all_gather(small, "ctx", axis=0, tiled=False, axis_index_groups=runs)
    small, low = lax.optimization_barrier((small, low))
    small = jnp.stack([small, swap(small, across)])
    small_other = swap(small, 1)

    low = jnp.stack([low, swap(low, across)])
    local = jnp.concatenate([frozen_query, output_gradient], axis=0)
    local, _ = lax.optimization_barrier((local, kv))
    pair = jnp.stack([local, swap(local, across)])
    ints = jnp.concatenate(
        [document_index.reshape(1, rows), jnp.pad(routes, ((0, 7 - 1), (0, rows - 2)))], axis=0
    )
    ints, _ = lax.optimization_barrier((ints, kv))
    ints = jnp.stack([ints, swap(ints, across)])
    meta = jnp.stack(
        [
            place // across,
            place // 2 % z_count,
            place % 2,
            ints[0, 1, 0],
            ints[0, 1, 1],
            ints[1, 1, 0],
            ints[1, 1, 1],
        ]
    ).astype(jnp.int32)
    side = pl.pallas_call(
        functools.partial(prepare, heads, z_count),
        out_shape=jax.ShapeDtypeStruct((2, SIDE, HEAD), bf16),
        in_specs=[smem] + [vmem] * 5,
        out_specs=vmem,
    )(meta, small, small_other, low, pair, ints)
    own, side = lax.optimization_barrier((own, side))
    other = swap(own, 1)
    quads = z_count // 2
    prob, out, stats = pl.pallas_call(
        functools.partial(forward, heads, z_count),
        out_shape=(
            jax.ShapeDtypeStruct((2, quads, QUAD, stack), bf16),
            jax.ShapeDtypeStruct((2, HEAD, stack), f32),
            jax.ShapeDtypeStruct((2, 8, stack), f32),
        ),
        in_specs=[smem] + [vmem] * 3,
        out_specs=(vmem,) * 3,
        scratch_shapes=[pltpu.VMEM((quads, QUAD, stack), f32)],
        compiler_params=pltpu.CompilerParams(vmem_limit_bytes=30 * 1024 * 1024),
    )(meta, own, other, side)
    come = swap(jnp.where(place < across, stats[1], stats[0]), across)

    send = jax.ShapeDtypeStruct((z_count, GRAD, HEAD), bf16)
    dquery, dquery_across, send_own, send_other = pl.pallas_call(
        functools.partial(backward, heads, z_count),
        out_shape=(
            jax.ShapeDtypeStruct((rows, wide), f32),
            jax.ShapeDtypeStruct((rows, wide), bf16),
            send,
            send,
        ),
        in_specs=[smem] + [vmem] * 6,
        out_specs=(vmem,) * 4,
        scratch_shapes=[
            pltpu.VMEM((z_count, GRAD, HEAD), f32),
            pltpu.VMEM((z_count, GRAD, HEAD), f32),
            pltpu.VMEM((stack, HEAD), bf16),
        ],
        compiler_params=pltpu.CompilerParams(vmem_limit_bytes=30 * 1024 * 1024),
    )(meta, own, other, side, prob, stats, come)

    chip = send_own + swap(send_other, 1)
    part = lax.psum_scatter(
        chip, "ctx", scatter_dimension=0, tiled=False, axis_index_groups=runs
    )

    far_out = jnp.where(place < across, out[1], out[0]).astype(bf16)
    far, _ = lax.optimization_barrier((jnp.stack([far_out, dquery_across.reshape(HEAD, stack)]), chip))
    far = swap(far, across)
    attended, dquery = pl.pallas_call(
        functools.partial(finish, heads),
        out_shape=(jax.ShapeDtypeStruct((rows, wide), f32),) * 2,
        in_specs=[smem] + [vmem] * 6,
        out_specs=(vmem,) * 2,
    )(meta, out, stats, come, far[0], far[1].reshape(rows, wide), dquery)

    up_grad = part[KV : KV + UPS].astype(f32) + swap(part[KV + UPS :], across).astype(f32)
    up_grad = up_grad.reshape(heads, up_rows, HEAD).transpose(1, 0, 2)
    return (
        attended,
        dquery,
        part[KEYS].astype(f32),
        part[VALUES].astype(f32),
        up_grad.reshape(up_rows, wide),
    )


def solution(mesh):
    both = P("ctx", "exp")
    return jax.shard_map(
        shards,
        mesh=mesh,
        in_specs=(
            both,
            both,
            both,
            both,
            P("ctx"),
            P("ctx", None),
            P(None, "exp", None),
            both,
            both,
        ),
        out_specs=(both,) * 5,
        check_vma=False,
    )
```

```python
import functools
import math

import jax
import jax.numpy as jnp
from jax import lax
from jax.experimental import pallas as pl
from jax.experimental.pallas import tpu as pltpu
from jax.sharding import PartitionSpec as P

HEAD = 128
RANK = 64
BLOCK = 128
QUAD = 4 * BLOCK

adapter_scale = 0.5
far_below = -1e30
to_two = math.log2(math.e) / math.sqrt(HEAD)
inverse = 1.0 / math.sqrt(HEAD)
f32 = jnp.float32
bf16 = jnp.bfloat16

KV = 2 * BLOCK
UPS = 64
GRAD = KV + 2 * UPS
SMALL = UPS + 16

STACK = 4 * BLOCK
GOUT_AT, LOW_AT, START_AT = STACK, 2 * STACK, 2 * STACK + BLOCK
SIDE = START_AT + 16
KEYS, VALUES = slice(0, BLOCK), slice(BLOCK, KV)


def last_last(a, b):
    return lax.dot_general(a, b, (((1,), (1,)), ((), ())), preferred_element_type=f32)


def first_first(a, b):
    return lax.dot_general(a, b, (((0,), (0,)), ((), ())), preferred_element_type=f32)


def plain(a, b):
    return lax.dot_general(a, b, (((1,), (0,)), ((), ())), preferred_element_type=f32)


def sum_low(lows, low_out):
    low = lows[0]
    for i in range(1, lows.shape[0]):
        low = low + lows[i]
    low_out[...] = low.astype(bf16)


def expert_at(meta, z_count, w, j):
    first = meta[3 + 2 * w + j] * 4
    return lax.rem(first, 2 * z_count) // 2, lax.div(first, 2 * z_count) ^ meta[0]


def query_base(meta, z_count, w):
    yh, z, core = meta[0], meta[1], meta[2]
    across = (1 - 2 * yh) * 2 * z_count * BLOCK
    return (2 * z + core) * BLOCK + w * across


def quad_range(meta, z_count, w, start):
    base = query_base(meta, z_count, w)
    first_key = jnp.min(start.astype(f32)).astype(jnp.int32)
    first = jnp.clip(first_key, 0, z_count * KV) // QUAD
    last = jnp.clip(base, -QUAD, z_count * KV - 1) // QUAD
    last = jnp.where(base < 0, -1, last)
    return first, last


def prepare(heads, z_count, meta, own, other, low_ref, pair, docs, side):
    core = meta[2]

    counts = jnp.zeros((16, 128), f32)
    for i in range(z_count):
        for slot in range(2):
            for ref in (own, other):
                counts += ref[slot, i, UPS:SMALL, :].astype(f32)
    high = jnp.floor(counts * (1.0 / 128.0))
    rest = (counts - 128.0 * high).astype(bf16)
    high = high.astype(bf16)
    lane = lax.broadcasted_iota(jnp.int32, (128, BLOCK), 0)

    for w in range(2):
        low = low_ref[w]
        side[w, LOW_AT:START_AT, :] = low
        for h in range(heads):
            columns = slice(h * HEAD, (h + 1) * HEAD)
            rows = []
            for j in range(2):
                z_at, slot = expert_at(meta, z_count, w, j)
                at = slice(16 * h, 16 * h + 16)
                for step in range(2):
                    mine, theirs = own[slot, z_at + step, at, :], other[slot, z_at + step, at, :]
                    rows.append(jnp.where(core == 0, mine, theirs))
                    rows.append(jnp.where(core == 0, theirs, mine))
            delta = plain(low, jnp.concatenate(rows, axis=0))
            side[w, h * BLOCK : (h + 1) * BLOCK, :] = (
                pair[w, 0:BLOCK, columns].astype(f32) + adapter_scale * delta
            ).astype(bf16)
            gout = pair[w, BLOCK : 2 * BLOCK, columns].astype(f32).T
            side[w, GOUT_AT + h * HEAD : GOUT_AT + (h + 1) * HEAD, :] = gout.astype(bf16)
        pick = jnp.where(lane == docs[w, 0:1, :], 1.0, 0.0).astype(bf16)
        whole = jnp.sum(plain(high, pick), axis=0, keepdims=True)
        part = jnp.sum(plain(rest, pick), axis=0, keepdims=True)
        side[w, START_AT:SIDE, :] = jnp.concatenate(
            [whole, part, jnp.zeros((14, BLOCK), f32)], axis=0
        ).astype(bf16)


def start_of(meta, z_count, side, w):
    rows = side[w, START_AT:SIDE, :].astype(f32)
    start = 128.0 * rows[0:1] + rows[1:2]
    return start.astype(jnp.int32) - meta[0] * (z_count * KV)


def gout_of(heads, side, w):
    blocks = [side[w, GOUT_AT + h * HEAD : GOUT_AT + (h + 1) * HEAD, :] for h in range(heads)]
    return jnp.concatenate(blocks, axis=1).astype(f32)


def chip_pieces(core, own, other, quad):
    z_at = quad * 2
    return [
        (own, z_at, core),
        (other, z_at, 1 - core),
        (own, z_at + 1, 2 + core),
        (other, z_at + 1, 3 - core),
    ]


def rows_of(n):
    return slice(n * BLOCK, (n + 1) * BLOCK)


def forward(heads, z_count, meta, own, other, side, prob, out_ref, stats, score):
    wide = heads * BLOCK
    core = meta[2]
    ramp = lax.broadcasted_iota(jnp.int32, (BLOCK, wide), 0)

    for w in range(2):
        start = start_of(meta, z_count, side, w)
        whole_key = jnp.max(start.astype(f32)).astype(jnp.int32)
        first_quad, last_quad = quad_range(meta, z_count, w, start)
        start = jnp.concatenate([start] * heads, axis=1)
        place = query_base(meta, z_count, w) + lax.broadcasted_iota(jnp.int32, (1, BLOCK), 1)
        place = jnp.concatenate([place] * heads, axis=1)
        whole_key = jnp.clip(whole_key, 0, z_count * KV)
        whole_quad = jnp.minimum(
            jnp.maximum((whole_key + QUAD - 1) // QUAD, first_quad), last_quad
        )
        queries = side[w, 0:STACK, :]

        def scores(masked, quad, top):
            for n, (src, z_at, at) in enumerate(chip_pieces(core, own, other, quad)):
                s = last_last(src[z_at, KEYS, :], queries)
                if masked:
                    base = quad * QUAD + at * BLOCK
                    s = jnp.where((ramp >= start - base) & (ramp <= place - base), s, far_below)
                score[quad, rows_of(n), :] = s
                top = jnp.maximum(top, jnp.max(s.reshape(BLOCK // 8, 8, wide), axis=0))
            return top

        top = jnp.full((8, wide), far_below, f32)
        top = lax.fori_loop(
            first_quad,
            jnp.where(last_quad >= first_quad, whole_quad + 1, first_quad),
            lambda i, t: scores(True, jnp.where(i == whole_quad, last_quad, i), t),
            top,
        )
        top = lax.fori_loop(
            jnp.maximum(whole_quad, first_quad),
            last_quad,
            functools.partial(scores, False),
            top,
        )
        top = jnp.max(top, axis=0, keepdims=True)
        top = jnp.where(top < 0.5 * far_below, 0.0, top)

        def attend(quad, carry):
            total, out = carry
            values = []
            for n, (src, z_at, _) in enumerate(chip_pieces(core, own, other, quad)):
                p = jnp.exp2((score[quad, rows_of(n), :] - top) * to_two)
                total = total + jnp.sum(p.reshape(BLOCK // 8, 8, wide), axis=0)
                prob[w, quad, rows_of(n), :] = p.astype(bf16)
                values.append(src[z_at, VALUES, :])
            out = out + first_first(jnp.concatenate(values, axis=0), prob[w, quad])
            return total, out

        total, out = lax.fori_loop(
            first_quad,
            last_quad + 1,
            attend,
            (jnp.zeros((8, wide), f32), jnp.zeros((HEAD, wide), f32)),
        )
        total = jnp.sum(total, axis=0, keepdims=True)
        some = total > 0.0
        safe = jnp.where(some, total, 1.0)
        out = out * (1.0 / safe)
        out_ref[w] = out
        row_delta = jnp.sum(gout_of(heads, side, w) * out, axis=0, keepdims=True)
        log_top = top * to_two
        log_sum = jnp.where(some, log_top + jnp.log2(safe), far_below)
        filled = jnp.where(some, 1.0, 0.0)
        stats[w] = jnp.concatenate(
            [log_sum, row_delta, log_top, filled, jnp.zeros((4, wide), f32)], axis=0
        )


def shares(log_sum, far_log, crossed):
    far_log = jnp.where(crossed, far_log, far_below)
    most = jnp.maximum(log_sum, far_log)
    log_all = most + jnp.log2(jnp.exp2(log_sum - most) + jnp.exp2(far_log - most))
    far = jnp.where(crossed, jnp.exp2(far_log - log_all), 0.0)
    return log_all, jnp.exp2(log_sum - log_all), far


def backward(
    heads,
    z_count,
    meta,
    own,
    other,
    side,
    prob,
    stats,
    come,
    dquery,
    dquery_across,
    send_own,
    send_other,
    sum_own,
    sum_other,
    gscaled,
):
    wide = heads * BLOCK
    yh, core = meta[0], meta[2]
    sum_own[...] = jnp.zeros(sum_own.shape, f32)
    sum_other[...] = jnp.zeros(sum_other.shape, f32)

    for w in range(2):
        log_sum, row_delta, log_top, filled = (stats[w, i : i + 1, :] for i in range(4))
        log_all, near, far = shares(log_sum, come[0:1, :], (1 - yh) == w)
        scale = jnp.where(filled > 0.0, jnp.exp2(log_top - log_all), 0.0)
        delta = (row_delta * near + come[1:2, :] * far) * scale
        gout = gout_of(heads, side, w) * scale
        for h in range(heads):
            columns = slice(h * HEAD, (h + 1) * HEAD)
            gscaled[h * BLOCK : (h + 1) * BLOCK, :] = gout[:, columns].T.astype(bf16)
        grads = gscaled[...]
        queries = side[w, 0:STACK, :]
        first_quad, last_quad = quad_range(
            meta, z_count, w, start_of(meta, z_count, side, w)
        )

        def step(quad, dq):
            keys, dscores = [], []
            places = chip_pieces(core, (own, sum_own), (other, sum_other), quad)
            for n, ((src, dst), z_at, _) in enumerate(places):
                p = prob[w, quad, rows_of(n), :]
                dp = last_last(src[z_at, VALUES, :], grads)
                ds = (p.astype(f32) * (dp - delta)).astype(bf16)
                dst[z_at, KEYS, :] += plain(ds, queries)
                dst[z_at, VALUES, :] += plain(p, grads)
                keys.append(src[z_at, KEYS, :])
                dscores.append(ds)
            return dq + first_first(
                jnp.concatenate(keys, axis=0), jnp.concatenate(dscores, axis=0)
            )

        dq = lax.fori_loop(first_quad, last_quad + 1, step, jnp.zeros((HEAD, wide), f32))
        dq = dq * inverse
        low = side[w, LOW_AT:START_AT, :]
        for h in range(heads):
            columns = slice(h * HEAD, (h + 1) * HEAD)
            dq_h = dq[:, columns].T
            dq_low = dq_h.astype(bf16)
            if w == 0:
                dquery[:, columns] = dq_h
            else:
                dquery_across[:, columns] = dq_low
            up = adapter_scale * first_first(low, dq_low)
            for j in range(2):
                z_at, slot = expert_at(meta, z_count, w, j)
                at = pl.ds(pl.multiple_of(KV + slot * UPS + 16 * h, 16), 16)
                for i in range(2):
                    row = j * RANK + 32 * i
                    even, odd = up[row : row + 16, :], up[row + 16 : row + 32, :]
                    sum_own[z_at + i, at, :] += jnp.where(core == 0, even, odd)
                    sum_other[z_at + i, at, :] += jnp.where(core == 0, odd, even)

    for src, dst in ((sum_own, send_own), (sum_other, send_other)):
        dst[:, KEYS, :] = (src[:, KEYS, :] * inverse).astype(bf16)
        dst[:, BLOCK:GRAD, :] = src[:, BLOCK:GRAD, :].astype(bf16)


def finish(heads, meta, out_t, stats, come, far_out, far_dquery, dquery, attended, dquery_out):
    _, near, far = shares(stats[0, 0:1, :], come[0:1, :], meta[0] == 1)
    out = out_t[0] * near + far_out[...].astype(f32) * far
    for h in range(heads):
        columns = slice(h * HEAD, (h + 1) * HEAD)
        attended[:, columns] = out[:, columns].T
    dquery_out[...] = dquery[...] + far_dquery[...].astype(f32)


def swap(array, distance):
    count = lax.axis_size("ctx")
    return lax.ppermute(array, "ctx", [(i, i ^ distance) for i in range(count)])


def shards(
    normed,
    frozen_query,
    input_keys,
    input_values,
    document_index,
    routes,
    adapter_down_weight,
    adapter_up_weight,
    output_gradient,
):
    z_count = lax.axis_size("ctx") // 4
    across = 2 * z_count
    exp_count = lax.axis_size("exp")
    place = lax.axis_index("ctx")
    runs = [
        [(yh * z_count + z) * 2 + core for z in range(z_count)]
        for yh in range(2)
        for core in range(2)
    ]
    rows = normed.shape[0]
    wide = frozen_query.shape[1]
    heads = wide // HEAD
    stack = heads * rows
    up_rows = adapter_up_weight.shape[0]
    vmem = pl.BlockSpec(memory_space=pltpu.VMEM)
    smem = pl.BlockSpec(memory_space=pltpu.SMEM)

    kv = jnp.concatenate([input_keys, input_values], axis=0)
    own = lax.all_gather(kv, "ctx", axis=0, tiled=False, axis_index_groups=runs)

    chosen = [
        lax.dynamic_index_in_dim(adapter_down_weight, routes[0, j], 0, keepdims=False)
        for j in range(2)
    ]
    partial = jnp.dot(normed, jnp.concatenate(chosen, axis=1), preferred_element_type=f32)
    spread = jnp.broadcast_to(partial[None], (exp_count,) + partial.shape)
    lows = lax.all_to_all(spread, "exp", 0, 0)
    low = pl.pallas_call(
        sum_low,
        out_shape=jax.ShapeDtypeStruct(partial.shape, bf16),
        in_specs=[vmem],
        out_specs=vmem,
    )(lows)
    local = jnp.concatenate([frozen_query, output_gradient], axis=0)
    ints = jnp.concatenate(
        [document_index.reshape(1, rows), jnp.pad(routes, ((0, 6), (0, rows - 2)))], axis=0
    )
    local, ints, _ = lax.optimization_barrier((local, ints, kv))

    ups = adapter_up_weight.reshape(up_rows, heads, HEAD).transpose(1, 0, 2)
    ups = ups.reshape(up_rows * heads, HEAD)
    lower = document_index[:, None] < jnp.arange(128, dtype=jnp.int32)[None, :]
    counts = jnp.sum(lower.astype(f32), axis=0, keepdims=True).astype(bf16)
    small = jnp.concatenate([ups, jnp.pad(counts, ((0, 15), (0, 0)))], axis=0)
    small, _ = lax.optimization_barrier((small, (kv, spread, local, ints)))
    small = lax.all_gather(small, "ctx", axis=0, tiled=False, axis_index_groups=runs)
    small, low, local_far, ints_far = lax.optimization_barrier(
        (small, low, swap(local, across), swap(ints, across))
    )
    pair, ints = jnp.stack([local, local_far]), jnp.stack([ints, ints_far])
    small = jnp.stack([small, swap(small, across)])
    low = jnp.stack([low, swap(low, across)])
    small, low = lax.optimization_barrier((small, low))
    small_other = swap(small, 1)

    meta = jnp.stack(
        [
            place // across,
            place // 2 % z_count,
            place % 2,
            ints[0, 1, 0],
            ints[0, 1, 1],
            ints[1, 1, 0],
            ints[1, 1, 1],
        ]
    ).astype(jnp.int32)
    side = pl.pallas_call(
        functools.partial(prepare, heads, z_count),
        out_shape=jax.ShapeDtypeStruct((2, SIDE, HEAD), bf16),
        in_specs=[smem] + [vmem] * 5,
        out_specs=vmem,
    )(meta, small, small_other, low, pair, ints)
    own, side = lax.optimization_barrier((own, side))
    other = swap(own, 1)
    quads = z_count // 2
    prob, out, stats = pl.pallas_call(
        functools.partial(forward, heads, z_count),
        out_shape=(
            jax.ShapeDtypeStruct((2, quads, QUAD, stack), bf16),
            jax.ShapeDtypeStruct((2, HEAD, stack), f32),
            jax.ShapeDtypeStruct((2, 8, stack), f32),
        ),
        in_specs=[smem] + [vmem] * 3,
        out_specs=(vmem,) * 3,
        scratch_shapes=[pltpu.VMEM((quads, QUAD, stack), f32)],
        compiler_params=pltpu.CompilerParams(vmem_limit_bytes=30 * 1024 * 1024),
    )(meta, own, other, side)
    come = swap(jnp.where(place < across, stats[1], stats[0]), across)

    send = jax.ShapeDtypeStruct((z_count, GRAD, HEAD), bf16)
    dquery, dquery_across, send_own, send_other = pl.pallas_call(
        functools.partial(backward, heads, z_count),
        out_shape=(
            jax.ShapeDtypeStruct((rows, wide), f32),
            jax.ShapeDtypeStruct((rows, wide), bf16),
            send,
            send,
        ),
        in_specs=[smem] + [vmem] * 6,
        out_specs=(vmem,) * 4,
        scratch_shapes=[
            pltpu.VMEM((z_count, GRAD, HEAD), f32),
            pltpu.VMEM((z_count, GRAD, HEAD), f32),
            pltpu.VMEM((stack, HEAD), bf16),
        ],
        compiler_params=pltpu.CompilerParams(vmem_limit_bytes=30 * 1024 * 1024),
    )(meta, own, other, side, prob, stats, come)

    chip = send_own + swap(send_other, 1)
    part = lax.psum_scatter(
        chip, "ctx", scatter_dimension=0, tiled=False, axis_index_groups=runs
    )

    far_out = jnp.where(place < across, out[1], out[0]).astype(bf16)
    far, _ = lax.optimization_barrier((jnp.stack([far_out, dquery_across.reshape(HEAD, stack)]), chip))
    far = swap(far, across)
    attended, dquery = pl.pallas_call(
        functools.partial(finish, heads),
        out_shape=(jax.ShapeDtypeStruct((rows, wide), f32),) * 2,
        in_specs=[smem] + [vmem] * 6,
        out_specs=(vmem,) * 2,
    )(meta, out, stats, come, far[0], far[1].reshape(rows, wide), dquery)

    up_grad = part[KV : KV + UPS].astype(f32) + swap(part[KV + UPS :], across).astype(f32)
    up_grad = up_grad.reshape(heads, up_rows, HEAD).transpose(1, 0, 2)
    return (
        attended,
        dquery,
        part[KEYS].astype(f32),
        part[VALUES].astype(f32),
        up_grad.reshape(up_rows, wide),
    )


def solution(mesh):
    both = P("ctx", "exp")
    return jax.shard_map(
        shards,
        mesh=mesh,
        in_specs=(
            both,
            both,
            both,
            both,
            P("ctx"),
            P("ctx", None),
            P(None, "exp", None),
            both,
            both,
        ),
        out_specs=(both,) * 5,
        check_vma=False,
    )
```

```python
import functools
import math

import jax
import jax.numpy as jnp
from jax import lax
from jax.experimental import pallas as pl
from jax.experimental.pallas import tpu as pltpu
from jax.sharding import PartitionSpec as P

HEAD = 128
RANK = 64
BLOCK = 128
QUAD = 4 * BLOCK

adapter_scale = 0.5
far_below = -1e30
to_two = math.log2(math.e) / math.sqrt(HEAD)
inverse = 1.0 / math.sqrt(HEAD)
f32 = jnp.float32
bf16 = jnp.bfloat16

KV = 2 * BLOCK
UPS = 64
GRAD = KV + 2 * UPS
SMALL = UPS + 16

STACK = 4 * BLOCK
GOUT_AT, LOW_AT, START_AT = STACK, 2 * STACK, 2 * STACK + BLOCK
SIDE = START_AT + 16
KEYS, VALUES = slice(0, BLOCK), slice(BLOCK, KV)


def last_last(a, b):
    return lax.dot_general(a, b, (((1,), (1,)), ((), ())), preferred_element_type=f32)


def first_first(a, b):
    return lax.dot_general(a, b, (((0,), (0,)), ((), ())), preferred_element_type=f32)


def plain(a, b):
    return lax.dot_general(a, b, (((1,), (0,)), ((), ())), preferred_element_type=f32)


def sum_low(lows, low_out):
    low = lows[0]
    for i in range(1, lows.shape[0]):
        low = low + lows[i]
    low_out[...] = low.astype(bf16)


def expert_at(meta, ids, z_count, w, j):
    first = ids[w, 1, j] * 4
    return lax.rem(first, 2 * z_count) // 2, lax.div(first, 2 * z_count) ^ meta[0]


def query_base(meta, z_count, w):
    yh, z, core = meta[0], meta[1], meta[2]
    across = (1 - 2 * yh) * 2 * z_count * BLOCK
    return (2 * z + core) * BLOCK + w * across


def quad_range(meta, z_count, w, start):
    base = query_base(meta, z_count, w)
    first_key = jnp.min(start.astype(f32)).astype(jnp.int32)
    first = jnp.clip(first_key, 0, z_count * KV) // QUAD
    last = jnp.clip(base, -QUAD, z_count * KV - 1) // QUAD
    last = jnp.where(base < 0, -1, last)
    return first, last


def prepare(heads, z_count, meta, ids, own, other, low_ref, pair, docs, side):
    core = meta[2]

    counts = jnp.zeros((16, 128), f32)
    for i in range(z_count):
        for slot in range(2):
            for ref in (own, other):
                counts += ref[slot, i, UPS:SMALL, :].astype(f32)
    high = jnp.floor(counts * (1.0 / 128.0))
    rest = (counts - 128.0 * high).astype(bf16)
    high = high.astype(bf16)
    lane = lax.broadcasted_iota(jnp.int32, (128, BLOCK), 0)

    for w in range(2):
        low = low_ref[w]
        side[w, LOW_AT:START_AT, :] = low
        for h in range(heads):
            columns = slice(h * HEAD, (h + 1) * HEAD)
            rows = []
            for j in range(2):
                z_at, slot = expert_at(meta, ids, z_count, w, j)
                at = slice(16 * h, 16 * h + 16)
                for step in range(2):
                    mine, theirs = own[slot, z_at + step, at, :], other[slot, z_at + step, at, :]
                    rows.append(jnp.where(core == 0, mine, theirs))
                    rows.append(jnp.where(core == 0, theirs, mine))
            delta = plain(low, jnp.concatenate(rows, axis=0))
            side[w, h * BLOCK : (h + 1) * BLOCK, :] = (
                pair[w, 0:BLOCK, columns].astype(f32) + adapter_scale * delta
            ).astype(bf16)
            gout = pair[w, BLOCK : 2 * BLOCK, columns].astype(f32).T
            side[w, GOUT_AT + h * HEAD : GOUT_AT + (h + 1) * HEAD, :] = gout.astype(bf16)
        pick = jnp.where(lane == docs[w, 0:1, :], 1.0, 0.0).astype(bf16)
        whole = jnp.sum(plain(high, pick), axis=0, keepdims=True)
        part = jnp.sum(plain(rest, pick), axis=0, keepdims=True)
        side[w, START_AT:SIDE, :] = jnp.concatenate(
            [whole, part, jnp.zeros((14, BLOCK), f32)], axis=0
        ).astype(bf16)


def start_of(meta, z_count, side, w):
    rows = side[w, START_AT:SIDE, :].astype(f32)
    start = 128.0 * rows[0:1] + rows[1:2]
    return start.astype(jnp.int32) - meta[0] * (z_count * KV)


def gout_of(heads, side, w):
    blocks = [side[w, GOUT_AT + h * HEAD : GOUT_AT + (h + 1) * HEAD, :] for h in range(heads)]
    return jnp.concatenate(blocks, axis=1).astype(f32)


def chip_pieces(core, own, other, quad):
    z_at = quad * 2
    return [
        (own, z_at, core),
        (other, z_at, 1 - core),
        (own, z_at + 1, 2 + core),
        (other, z_at + 1, 3 - core),
    ]


def rows_of(n):
    return slice(n * BLOCK, (n + 1) * BLOCK)


def forward(heads, z_count, meta, own, other, side, prob, out_ref, stats, score):
    wide = heads * BLOCK
    core = meta[2]
    ramp = lax.broadcasted_iota(jnp.int32, (BLOCK, wide), 0)

    for w in range(2):
        start = start_of(meta, z_count, side, w)
        whole_key = jnp.max(start.astype(f32)).astype(jnp.int32)
        first_quad, last_quad = quad_range(meta, z_count, w, start)
        start = jnp.concatenate([start] * heads, axis=1)
        place = query_base(meta, z_count, w) + lax.broadcasted_iota(jnp.int32, (1, BLOCK), 1)
        place = jnp.concatenate([place] * heads, axis=1)
        whole_key = jnp.clip(whole_key, 0, z_count * KV)
        whole_quad = jnp.minimum(
            jnp.maximum((whole_key + QUAD - 1) // QUAD, first_quad), last_quad
        )
        queries = side[w, 0:STACK, :]

        def scores(masked, quad, top):
            for n, (src, z_at, at) in enumerate(chip_pieces(core, own, other, quad)):
                s = last_last(src[z_at, KEYS, :], queries)
                if masked:
                    base = quad * QUAD + at * BLOCK
                    s = jnp.where((ramp >= start - base) & (ramp <= place - base), s, far_below)
                score[quad, rows_of(n), :] = s
                top = jnp.maximum(top, jnp.max(s.reshape(BLOCK // 8, 8, wide), axis=0))
            return top

        top = jnp.full((8, wide), far_below, f32)
        top = lax.fori_loop(
            first_quad,
            jnp.where(last_quad >= first_quad, whole_quad + 1, first_quad),
            lambda i, t: scores(True, jnp.where(i == whole_quad, last_quad, i), t),
            top,
        )
        top = lax.fori_loop(
            jnp.maximum(whole_quad, first_quad),
            last_quad,
            functools.partial(scores, False),
            top,
        )
        top = jnp.max(top, axis=0, keepdims=True)
        top = jnp.where(top < 0.5 * far_below, 0.0, top)

        def attend(quad, carry):
            total, out = carry
            values = []
            for n, (src, z_at, _) in enumerate(chip_pieces(core, own, other, quad)):
                p = jnp.exp2((score[quad, rows_of(n), :] - top) * to_two)
                total = total + jnp.sum(p.reshape(BLOCK // 8, 8, wide), axis=0)
                prob[w, quad, rows_of(n), :] = p.astype(bf16)
                values.append(src[z_at, VALUES, :])
            out = out + first_first(jnp.concatenate(values, axis=0), prob[w, quad])
            return total, out

        total, out = lax.fori_loop(
            first_quad,
            last_quad + 1,
            attend,
            (jnp.zeros((8, wide), f32), jnp.zeros((HEAD, wide), f32)),
        )
        total = jnp.sum(total, axis=0, keepdims=True)
        some = total > 0.0
        safe = jnp.where(some, total, 1.0)
        out = out * (1.0 / safe)
        out_ref[w] = out
        row_delta = jnp.sum(gout_of(heads, side, w) * out, axis=0, keepdims=True)
        log_top = top * to_two
        log_sum = jnp.where(some, log_top + jnp.log2(safe), far_below)
        filled = jnp.where(some, 1.0, 0.0)
        stats[w] = jnp.concatenate(
            [log_sum, row_delta, log_top, filled, jnp.zeros((4, wide), f32)], axis=0
        )


def shares(log_sum, far_log, crossed):
    far_log = jnp.where(crossed, far_log, far_below)
    most = jnp.maximum(log_sum, far_log)
    log_all = most + jnp.log2(jnp.exp2(log_sum - most) + jnp.exp2(far_log - most))
    far = jnp.where(crossed, jnp.exp2(far_log - log_all), 0.0)
    return log_all, jnp.exp2(log_sum - log_all), far


def backward(
    heads,
    z_count,
    meta,
    ids,
    own,
    other,
    side,
    prob,
    stats,
    come,
    dquery,
    dquery_across,
    send_own,
    send_other,
    sum_own,
    sum_other,
    gscaled,
):
    wide = heads * BLOCK
    yh, core = meta[0], meta[2]
    sum_own[...] = jnp.zeros(sum_own.shape, f32)
    sum_other[...] = jnp.zeros(sum_other.shape, f32)

    for w in range(2):
        log_sum, row_delta, log_top, filled = (stats[w, i : i + 1, :] for i in range(4))
        log_all, near, far = shares(log_sum, come[0:1, :], (1 - yh) == w)
        scale = jnp.where(filled > 0.0, jnp.exp2(log_top - log_all), 0.0)
        delta = (row_delta * near + come[1:2, :] * far) * scale
        gout = gout_of(heads, side, w) * scale
        for h in range(heads):
            columns = slice(h * HEAD, (h + 1) * HEAD)
            gscaled[h * BLOCK : (h + 1) * BLOCK, :] = gout[:, columns].T.astype(bf16)
        grads = gscaled[...]
        queries = side[w, 0:STACK, :]
        first_quad, last_quad = quad_range(
            meta, z_count, w, start_of(meta, z_count, side, w)
        )

        def step(quad, dq):
            keys, dscores = [], []
            places = chip_pieces(core, (own, sum_own), (other, sum_other), quad)
            for n, ((src, dst), z_at, _) in enumerate(places):
                p = prob[w, quad, rows_of(n), :]
                dp = last_last(src[z_at, VALUES, :], grads)
                ds = (p.astype(f32) * (dp - delta)).astype(bf16)
                dst[z_at, KEYS, :] += plain(ds, queries)
                dst[z_at, VALUES, :] += plain(p, grads)
                keys.append(src[z_at, KEYS, :])
                dscores.append(ds)
            return dq + first_first(
                jnp.concatenate(keys, axis=0), jnp.concatenate(dscores, axis=0)
            )

        dq = lax.fori_loop(first_quad, last_quad + 1, step, jnp.zeros((HEAD, wide), f32))
        dq = dq * inverse
        low = side[w, LOW_AT:START_AT, :]
        for h in range(heads):
            columns = slice(h * HEAD, (h + 1) * HEAD)
            dq_h = dq[:, columns].T
            dq_low = dq_h.astype(bf16)
            if w == 0:
                dquery[:, columns] = dq_h
            else:
                dquery_across[:, columns] = dq_low
            up = adapter_scale * first_first(low, dq_low)
            for j in range(2):
                z_at, slot = expert_at(meta, ids, z_count, w, j)
                at = pl.ds(pl.multiple_of(KV + slot * UPS + 16 * h, 16), 16)
                for i in range(2):
                    row = j * RANK + 32 * i
                    even, odd = up[row : row + 16, :], up[row + 16 : row + 32, :]
                    sum_own[z_at + i, at, :] += jnp.where(core == 0, even, odd)
                    sum_other[z_at + i, at, :] += jnp.where(core == 0, odd, even)

    for src, dst in ((sum_own, send_own), (sum_other, send_other)):
        dst[:, KEYS, :] = (src[:, KEYS, :] * inverse).astype(bf16)
        dst[:, BLOCK:GRAD, :] = src[:, BLOCK:GRAD, :].astype(bf16)


def finish(heads, meta, out_t, stats, come, far_out, far_dquery, dquery, attended, dquery_out):
    _, near, far = shares(stats[0, 0:1, :], come[0:1, :], meta[0] == 1)
    out = out_t[0] * near + far_out[...].astype(f32) * far
    for h in range(heads):
        columns = slice(h * HEAD, (h + 1) * HEAD)
        attended[:, columns] = out[:, columns].T
    dquery_out[...] = dquery[...] + far_dquery[...].astype(f32)


def swap(array, distance):
    count = lax.axis_size("ctx")
    return lax.ppermute(array, "ctx", [(i, i ^ distance) for i in range(count)])


def shards(
    normed,
    frozen_query,
    input_keys,
    input_values,
    document_index,
    routes,
    adapter_down_weight,
    adapter_up_weight,
    output_gradient,
):
    z_count = lax.axis_size("ctx") // 4
    across = 2 * z_count
    exp_count = lax.axis_size("exp")
    place = lax.axis_index("ctx")
    runs = [
        [(yh * z_count + z) * 2 + core for z in range(z_count)]
        for yh in range(2)
        for core in range(2)
    ]
    rows = normed.shape[0]
    wide = frozen_query.shape[1]
    heads = wide // HEAD
    stack = heads * rows
    up_rows = adapter_up_weight.shape[0]
    vmem = pl.BlockSpec(memory_space=pltpu.VMEM)
    smem = pl.BlockSpec(memory_space=pltpu.SMEM)

    kv = jnp.concatenate([input_keys, input_values], axis=0)
    own = lax.all_gather(kv, "ctx", axis=0, tiled=False, axis_index_groups=runs)

    chosen = [
        lax.dynamic_index_in_dim(adapter_down_weight, routes[0, j], 0, keepdims=False)
        for j in range(2)
    ]
    partial = jnp.dot(normed, jnp.concatenate(chosen, axis=1), preferred_element_type=f32)
    spread = jnp.broadcast_to(partial[None], (exp_count,) + partial.shape)
    lows = lax.all_to_all(spread, "exp", 0, 0)
    low = pl.pallas_call(
        sum_low,
        out_shape=jax.ShapeDtypeStruct(partial.shape, bf16),
        in_specs=[vmem],
        out_specs=vmem,
    )(lows)
    ups = adapter_up_weight.reshape(up_rows, heads, HEAD).transpose(1, 0, 2)
    ups = ups.reshape(up_rows * heads, HEAD)
    lower = document_index[:, None] < jnp.arange(128, dtype=jnp.int32)[None, :]
    counts = jnp.sum(lower.astype(f32), axis=0, keepdims=True).astype(bf16)
    small = jnp.concatenate([ups, jnp.pad(counts, ((0, 15), (0, 0)))], axis=0)
    small, _ = lax.optimization_barrier((small, (kv, spread)))
    small = lax.all_gather(small, "ctx", axis=0, tiled=False, axis_index_groups=runs)
    small, low = lax.optimization_barrier((small, low))
    small = jnp.stack([small, swap(small, across)])
    small_other = swap(small, 1)

    low = jnp.stack([low, swap(low, across)])
    local = jnp.concatenate([frozen_query, output_gradient], axis=0)
    local, _ = lax.optimization_barrier((local, kv))
    pair = jnp.stack([local, swap(local, across)])
    ints = jnp.concatenate(
        [document_index.reshape(1, rows), jnp.pad(routes, ((0, 7 - 1), (0, rows - 2)))], axis=0
    )
    ints, _ = lax.optimization_barrier((ints, kv))
    ints = jnp.stack([ints, swap(ints, across)])
    meta = jnp.stack(
        [
            place // across,
            place // 2 % z_count,
            place % 2,
        ]
    ).astype(jnp.int32)
    side = pl.pallas_call(
        functools.partial(prepare, heads, z_count),
        out_shape=jax.ShapeDtypeStruct((2, SIDE, HEAD), bf16),
        in_specs=[smem] * 2 + [vmem] * 5,
        out_specs=vmem,
    )(meta, ints, small, small_other, low, pair, ints)
    own, side = lax.optimization_barrier((own, side))
    other = swap(own, 1)
    quads = z_count // 2
    prob, out, stats = pl.pallas_call(
        functools.partial(forward, heads, z_count),
        out_shape=(
            jax.ShapeDtypeStruct((2, quads, QUAD, stack), bf16),
            jax.ShapeDtypeStruct((2, HEAD, stack), f32),
            jax.ShapeDtypeStruct((2, 8, stack), f32),
        ),
        in_specs=[smem] + [vmem] * 3,
        out_specs=(vmem,) * 3,
        scratch_shapes=[pltpu.VMEM((quads, QUAD, stack), f32)],
        compiler_params=pltpu.CompilerParams(vmem_limit_bytes=30 * 1024 * 1024),
    )(meta, own, other, side)
    come = swap(jnp.where(place < across, stats[1], stats[0]), across)

    send = jax.ShapeDtypeStruct((z_count, GRAD, HEAD), bf16)
    dquery, dquery_across, send_own, send_other = pl.pallas_call(
        functools.partial(backward, heads, z_count),
        out_shape=(
            jax.ShapeDtypeStruct((rows, wide), f32),
            jax.ShapeDtypeStruct((rows, wide), bf16),
            send,
            send,
        ),
        in_specs=[smem] * 2 + [vmem] * 6,
        out_specs=(vmem,) * 4,
        scratch_shapes=[
            pltpu.VMEM((z_count, GRAD, HEAD), f32),
            pltpu.VMEM((z_count, GRAD, HEAD), f32),
            pltpu.VMEM((stack, HEAD), bf16),
        ],
        compiler_params=pltpu.CompilerParams(vmem_limit_bytes=30 * 1024 * 1024),
    )(meta, ints, own, other, side, prob, stats, come)

    chip = send_own + swap(send_other, 1)
    part = lax.psum_scatter(
        chip, "ctx", scatter_dimension=0, tiled=False, axis_index_groups=runs
    )

    far_out = jnp.where(place < across, out[1], out[0]).astype(bf16)
    far, _ = lax.optimization_barrier((jnp.stack([far_out, dquery_across.reshape(HEAD, stack)]), chip))
    far = swap(far, across)
    attended, dquery = pl.pallas_call(
        functools.partial(finish, heads),
        out_shape=(jax.ShapeDtypeStruct((rows, wide), f32),) * 2,
        in_specs=[smem] + [vmem] * 6,
        out_specs=(vmem,) * 2,
    )(meta, out, stats, come, far[0], far[1].reshape(rows, wide), dquery)

    up_grad = part[KV : KV + UPS].astype(f32) + swap(part[KV + UPS :], across).astype(f32)
    up_grad = up_grad.reshape(heads, up_rows, HEAD).transpose(1, 0, 2)
    return (
        attended,
        dquery,
        part[KEYS].astype(f32),
        part[VALUES].astype(f32),
        up_grad.reshape(up_rows, wide),
    )


def solution(mesh):
    both = P("ctx", "exp")
    return jax.shard_map(
        shards,
        mesh=mesh,
        in_specs=(
            both,
            both,
            both,
            both,
            P("ctx"),
            P("ctx", None),
            P(None, "exp", None),
            both,
            both,
        ),
        out_specs=(both,) * 5,
        check_vma=False,
    )
```
